32 devices in a mesh: groups: 2 (over y), ctx: 4 (over z), head: 2 (over x), sub: 2 (over core).
Axes of the slice: x: 2, y: 2, z: 4, core: 2. Of those that a mesh axis runs over, the one named last changes fastest.
Arguments:
- query_nope: bfloat16 [4, 4, 128, 128], P(('groups', 'sub'), None, 'head'), parts along dimension 0, may hold values from -6 to 6
- query_rope: bfloat16 [4, 4, 128, 64], P(('groups', 'sub'), None, 'head'), parts along dimension 0, may hold values from -8 to 8
- latent_cache: bfloat16 [4, 16384, 576], P(('groups', 'sub'), 'ctx'), parts along dimension 0, may hold values from -12 to 12
- lengths: int32 [4], P(('groups', 'sub')), parts along dimension 0, may hold values from 2052 to 16384, as said below
- block_ids: int32 [4, 4, 32], P(('groups', 'sub')), parts along dimension 0, may hold values from 0 to 255, as said below
- key_absorb: bfloat16 [128, 128, 512], P('head', None, 'ctx'), may hold values from -0.5 to 0.5
- value_absorb: bfloat16 [128, 512, 128], P('head', 'ctx'), may hold values from -0.25 to 0.25
- output_weight: bfloat16 [16384, 7168], P('head', 'ctx'), may hold values from -0.375 to 0.375
Outputs:
- attended: bfloat16 [4, 4, 7168], P(('groups', 'sub'), None, ('ctx', 'head')), parts along dimension 0
The draws below stay inside these ranges and needn't reach their ends.
There are 2 independent parts, one for each index of `groups`. The reference program is written for one: setup_inputs(seed, part) draws one part's arguments, and reference() takes and returns one part's arrays. A program takes and returns all parts, laid end to end along the dimension named above; an argument that names none is the same for every part. Nothing has to cross between parts.
Inputs may be any that keep to these rules, and one draw needn't show every extreme that they name: `lengths`: every request with the greatest length 16384 exists in each draw. `block_ids`: the 32 ids of one query token are distinct, and each block holds a position p <= lengths[r] - 4; the block of position lengths[r] - 4 is always among them.
All inputs are finite; a program needn't handle non-finite values.
Results may differ from the reference program's by a relative error of at most 0.03.
Values may be sent and summed in bfloat16 or wider, within the bound.
No kernel may reach another device: no remote copies, remote signals or barrier semaphores. Data moves between devices by JAX's collectives and lax.ppermute only.
A program may use at most 128 MiB of HBM per device.

```python
import jax
import jax.numpy as jnp
from jax import lax

HEADS = 128
NOPE = 128
ROPE = 64
LAT = 512
VH = 128
D = 7168
DRAFT = 4
BLK = 64
TOPK = 32
REQ = 2
CTX = 16384
SEGMENTS_EACH = 256


def request_lengths(key):
    lowest = TOPK * BLK + DRAFT
    drawn = jax.random.randint(jax.random.fold_in(key, 101), (REQ,), lowest, CTX + 1)
    longest = jax.random.randint(jax.random.fold_in(key, 102), (), 0, REQ)
    return jnp.where(jnp.arange(REQ) == longest, CTX, drawn).astype(jnp.int32)


def draw_lengths(key, part):
    return request_lengths(key)


def draw_block_ids(key, part):
    request_len = request_lengths(key)
    key = jax.random.fold_in(key, 5)
    valid_count = (request_len - DRAFT) // BLK + 1
    stored_segment_number = jnp.arange(SEGMENTS_EACH, dtype=jnp.int32)[None, None, :]
    noise_perturbation = jax.random.randint(key, (REQ, DRAFT, SEGMENTS_EACH), 0, 2 * SEGMENTS_EACH)
    usable_segment_flags = stored_segment_number < valid_count[:, None, None]
    latest_segments = stored_segment_number >= (valid_count - 2)[:, None, None]
    urgency_extra = jnp.where(latest_segments, 8 * SEGMENTS_EACH, 0)
    segment_urgency = jnp.where(usable_segment_flags, noise_perturbation + 2 * stored_segment_number + 1 + urgency_extra, 0)
    composite = segment_urgency * SEGMENTS_EACH + stored_segment_number
    _, picked = lax.top_k(composite, TOPK)
    return picked.astype(jnp.int32)


def draw_query_rope(key, part):
    key = jax.random.fold_in(key, 7)
    array_shape = (REQ, DRAFT, HEADS, ROPE)
    values = jnp.clip(jax.random.normal(key, array_shape, jnp.float32), -4.0, 4.0)
    return values.astype(jnp.bfloat16)


def draw_latent_cache(key, part):
    key = jax.random.fold_in(key, 9)
    array_shape = (REQ, CTX, LAT + ROPE)
    values = jnp.clip(jax.random.normal(key, array_shape, jnp.float32), -6.0, 6.0)
    return values.astype(jnp.bfloat16)


def steps_of(own_key, extent, pieces, least, largest):
    gain, own = 1.0, jax.random.fold_in(own_key, 6)
    for axis_at, shards_of in pieces:
        draws = jnp.exp(jax.random.uniform(jax.random.fold_in(own, axis_at), (shards_of,), jnp.float32, least / len(pieces), largest / len(pieces)))
        gain = gain * jnp.repeat(draws, extent[axis_at] // shards_of).reshape([-1 if axis == axis_at else 1 for axis in range(len(extent))])
    return gain


def bell_draw(rng, extent, spread, bound, shards=(), kind=jnp.bfloat16):
    gain = steps_of(rng, extent, shards, -0.22, 0.18) if shards else 1.0
    result = jax.random.normal(rng, extent, jnp.float32) * spread * gain
    return jnp.minimum(jnp.maximum(result, -bound), bound).astype(kind)


def setup_inputs(seed: int = 0, part: int = 0) -> dict:
    seeds = jax.random.split(jax.random.key(seed), 9)
    part_keys = jax.random.split(jax.random.fold_in(seeds[8], part), 9)
    query_nope = bell_draw(part_keys[0], (REQ, DRAFT, HEADS, NOPE), 1.0, 6.0, ((0, 2), (2, 2)))
    query_rope = draw_query_rope(jax.random.fold_in(jax.random.fold_in(seeds[8], part), 71), part)
    latent_cache = draw_latent_cache(jax.random.fold_in(jax.random.fold_in(seeds[8], part), 71), part)
    lengths = draw_lengths(jax.random.fold_in(jax.random.fold_in(seeds[8], part), 71), part)
    block_ids = draw_block_ids(jax.random.fold_in(jax.random.fold_in(seeds[8], part), 71), part)
    key_absorb = bell_draw(seeds[5], (HEADS, NOPE, LAT), NOPE ** -0.5, 0.5, ((0, 2), (2, 4)))
    value_absorb = bell_draw(seeds[6], (HEADS, LAT, VH), LAT ** -0.5, 0.25, ((0, 2), (1, 4)))
    output_weight = bell_draw(seeds[7], (HEADS * VH, D), (HEADS * VH // 64) ** -0.5, 0.375, ((0, 2), (1, 4)))
    return {"query_nope": query_nope, "query_rope": query_rope, "latent_cache": latent_cache, "lengths": lengths, "block_ids": block_ids, "key_absorb": key_absorb, "value_absorb": value_absorb, "output_weight": output_weight}


def reference(query_nope, query_rope, latent_cache, lengths, block_ids, key_absorb, value_absorb, output_weight):
    softmax_scale = (NOPE + ROPE) ** -0.5
    q_latent = jnp.einsum('rtho,hoc->rthc', query_nope.astype(jnp.float32), key_absorb.astype(jnp.float32)).astype(jnp.bfloat16)
    queries = jnp.concatenate([q_latent, query_rope], axis=3)
    offsets = jnp.arange(BLK, dtype=jnp.int32)
    draft_steps = jnp.arange(DRAFT, dtype=jnp.int32)

    def one_request(request_items):
        query_rows, cache_rows, request_length, chosen_blocks = request_items
        token_ids = (chosen_blocks[:, :, None] * BLK + offsets[None, None, :]).reshape(DRAFT, TOPK * BLK)
        key_rows = jnp.take(cache_rows, token_ids, axis=0)
        visible = token_ids <= (request_length - DRAFT + draft_steps)[:, None]
        scores = jnp.einsum('thc,tsc->ths', query_rows.astype(jnp.float32), key_rows.astype(jnp.float32)) * softmax_scale
        scores = jnp.where(visible[:, None, :], scores, -1e30)
        row_max = jnp.max(scores, axis=2, keepdims=True)
        weights = jnp.where(visible[:, None, :], jnp.exp(scores - row_max), 0.0)
        denominator = jnp.sum(weights, axis=2, keepdims=True)
        rounded = lax.optimization_barrier(weights.astype(jnp.bfloat16))
        weighted = jnp.einsum('ths,tsc->thc', rounded.astype(jnp.float32), key_rows[:, :, :LAT].astype(jnp.float32))
        return (weighted / denominator).astype(jnp.bfloat16)

    o_latent = lax.map(one_request, (queries, latent_cache, lengths, block_ids))
    head_values = jnp.einsum('rthc,hcv->rthv', o_latent.astype(jnp.float32), value_absorb.astype(jnp.float32)).astype(jnp.bfloat16)
    flat_heads = head_values.reshape(REQ * DRAFT, HEADS * VH)
    attended = jnp.dot(flat_heads, output_weight, preferred_element_type=jnp.float32).astype(jnp.bfloat16)
    return attended.reshape(REQ, DRAFT, D)
```

```python
import jax
import jax.numpy as jnp
from jax import lax
from jax.sharding import PartitionSpec as P

BLK = 64
FEW = 4


def swap(value, axis, step):
    count = lax.axis_size(axis)
    return lax.ppermute(value, axis, [(i, i ^ step) for i in range(count)])


def everyone(value, axis):
    me, count = lax.axis_index(axis), lax.axis_size(axis)
    held = jnp.stack([value] + [swap(value, axis, step) for step in range(1, count)])
    return [held[me ^ i] for i in range(count)]


def halves(value):
    high = lax.reduce_precision(value, 8, 7)
    return high.astype(jnp.bfloat16), (value - high).astype(jnp.bfloat16)


def combine_few(local_max, total, weighted):
    me, count = lax.axis_index("ctx"), lax.axis_size("ctx")
    rows, width = weighted.shape
    part = width // count
    stats = jnp.stack([*halves(local_max), *halves(total)]).reshape(-1, part)

    def chunk(step):
        mine = lax.dynamic_slice(weighted, (0, (me ^ step) * part), (rows, part))
        return jnp.concatenate([mine.astype(jnp.bfloat16), stats], axis=0)

    held = [chunk(0)] + [swap(chunk(step), "ctx", step) for step in range(1, count)]
    maxima, totals, sums = [], [], []
    for packed in held:
        numbers = packed[rows:].astype(jnp.float32).reshape(4, rows)
        maxima.append(numbers[0] + numbers[1])
        totals.append(numbers[2] + numbers[3])
        sums.append(packed[:rows].astype(jnp.float32))
    joint = maxima[0]
    for other in maxima[1:]:
        joint = jnp.maximum(joint, other)
    factors = [jnp.exp(other - joint) for other in maxima]
    total = sum(a * b for a, b in zip(totals, factors))
    return sum(a * b[:, None] for a, b in zip(sums, factors)) / total[:, None]


def combine_many(local_max, total, weighted):
    joint = lax.pmax(local_max, "ctx")
    factor = jnp.exp(local_max - joint)
    total = lax.psum(total * factor, "ctx")
    summed = lax.psum_scatter(weighted * factor[:, None], "ctx", scatter_dimension=1, tiled=True)
    return summed / total[:, None]


def local(
    query_nope,
    query_rope,
    latent_cache,
    lengths,
    block_ids,
    key_absorb,
    value_absorb,
    output_weight,
):
    _, drafts, heads, nope = query_nope.shape
    rope = query_rope.shape[3]
    tokens = latent_cache.shape[1]
    scale = (nope + rope) ** (-0.5)
    rows = drafts * heads
    few = lax.axis_size("ctx") <= FEW

    q_piece = jnp.einsum(
        "tho,hoc->thc", query_nope[0], key_absorb, preferred_element_type=jnp.float32
    ).astype(jnp.bfloat16)
    if few:
        pieces = everyone(q_piece, "ctx")
    else:
        pieces = [lax.all_gather(q_piece, "ctx", axis=2, tiled=True)]
    queries = jnp.concatenate(pieces + [query_rope[0]], axis=2).reshape(rows, -1)
    latent = queries.shape[1] - rope

    cache = latent_cache[0]
    scores = jnp.einsum("qc,jc->qj", queries, cache, preferred_element_type=jnp.float32) * scale
    first = lax.axis_index("ctx") * tokens
    position = first + jnp.arange(tokens, dtype=jnp.int32)
    blocks = first // BLK + jnp.arange(tokens // BLK, dtype=jnp.int32)
    chosen = jnp.any(block_ids[0][:, :, None] == blocks[None, None, :], axis=1)
    limit = lengths[0] - drafts + jnp.arange(drafts, dtype=jnp.int32)
    visible = jnp.repeat(chosen, BLK, axis=1) & (position[None, :] <= limit[:, None])
    visible = jnp.broadcast_to(visible[:, None, :], (drafts, heads, tokens)).reshape(rows, tokens)
    scores = jnp.where(visible, scores, -1e30)
    local_max = jnp.max(scores, axis=1)
    weights = jnp.where(visible, jnp.exp(scores - local_max[:, None]), 0.0)
    total = jnp.sum(weights, axis=1)
    weighted = jnp.einsum(
        "qj,jc->qc",
        weights.astype(jnp.bfloat16),
        cache[:, :latent],
        preferred_element_type=jnp.float32,
    )

    combine = combine_few if few else combine_many
    o_latent = combine(local_max, total, weighted).astype(jnp.bfloat16)
    head_values = jnp.einsum(
        "thc,hcv->thv",
        o_latent.reshape(drafts, heads, -1),
        value_absorb,
        preferred_element_type=jnp.float32,
    )
    if few:
        piece = head_values.astype(jnp.bfloat16)
        head_values = piece.astype(jnp.float32)
        for step in range(1, lax.axis_size("ctx")):
            head_values += swap(piece, "ctx", step).astype(jnp.float32)
    else:
        head_values = lax.psum(head_values, "ctx")
    flat = head_values.astype(jnp.bfloat16).reshape(drafts, -1)
    partial = jnp.dot(flat, output_weight, preferred_element_type=jnp.float32)
    if lax.axis_size("head") == 2:
        me, half = lax.axis_index("head"), partial.shape[1] // 2
        mine = lax.dynamic_slice(partial, (0, me * half), (drafts, half))
        theirs = lax.dynamic_slice(partial, (0, (1 - me) * half), (drafts, half))
        summed = mine + swap(theirs, "head", 1)
    else:
        summed = lax.psum_scatter(partial, "head", scatter_dimension=1, tiled=True)
    return summed.astype(jnp.bfloat16)[None]


def solution(mesh):
    placed = (
        P(("groups", "sub"), None, "head", None),
        P(("groups", "sub"), None, "head", None),
        P(("groups", "sub"), "ctx", None),
        P(("groups", "sub")),
        P(("groups", "sub"), None, None),
        P("head", None, "ctx"),
        P("head", "ctx", None),
        P("head", "ctx"),
    )
    return jax.shard_map(
        local,
        mesh=mesh,
        in_specs=placed,
        out_specs=P(("groups", "sub"), None, ("ctx", "head")),
        check_vma=False,
    )
```

```python
import functools

import jax
import jax.numpy as jnp
from jax import lax
from jax.experimental import pallas as pl
from jax.experimental.pallas import tpu as pltpu
from jax.sharding import PartitionSpec as P

BLK = 64
FEW = 4
LANES = 128
TAIL = 16
LOG2E = 1.4426950408889634
HIDDEN = -1e30
MIB = 1024 * 1024
VMEM = pl.BlockSpec(memory_space=pltpu.VMEM)


def swap(value, axis, step):
    count = lax.axis_size(axis)
    return lax.ppermute(value, axis, [(i, i ^ step) for i in range(count)])


def thirds(value):
    high = value.astype(jnp.bfloat16)
    rest = value - high.astype(jnp.float32)
    middle = rest.astype(jnp.bfloat16)
    low = (rest - middle.astype(jnp.float32)).astype(jnp.bfloat16)
    return [part.astype(jnp.float32) for part in (high, middle, low)]


def attend_kernel(*refs, count, scale):
    pieces, (rope, cache, bias) = refs[:count], refs[count : count + 3]
    outs, (queries, total_sums) = refs[count + 3 : -2], refs[-2:]
    rows, width = pieces[0].shape
    latent = count * width
    me = lax.axis_index("ctx") if count > 1 else 0
    for step in range(count):
        at = pl.multiple_of((me ^ step) * width, width)
        queries[:, pl.ds(at, width)] = pieces[step][...]
    queries[:, latent:] = rope[...]

    tokens = cache.shape[1]
    scores = jnp.dot(queries[...], cache[...], preferred_element_type=jnp.float32)
    scores = (scores.reshape(rows // 8, 8, tokens) + bias[...][None]).reshape(rows, tokens)
    top = jnp.max(scores, axis=1, keepdims=True)
    weights = jnp.exp2((scores - top) * (scale * LOG2E))
    total = jnp.sum(weights, axis=1, keepdims=True)
    total_sums[...] = lax.dot_general(
        weights.astype(jnp.bfloat16),
        cache[:latent, :],
        (((1,), (1,)), ((), ())),
        preferred_element_type=jnp.float32,
    )

    lines = []
    for value in (top * scale, total):
        line = jnp.broadcast_to(value, (rows, LANES)).T[:1]
        for part in thirds(line):
            lines += [part[:, at : at + LANES] for at in range(0, rows, LANES)]
    lines.append(jnp.zeros((TAIL - len(lines), LANES), jnp.float32))
    tail = jnp.concatenate(lines, axis=0).astype(jnp.bfloat16)
    for step in range(count):
        at = pl.multiple_of((me ^ step) * width, width)
        outs[step][:rows, :] = total_sums[:, pl.ds(at, width)].astype(jnp.bfloat16)
        outs[step][rows:, :LANES] = tail


def attend(pieces, rope, cache, bias, scale):
    count, (rows, width) = len(pieces), pieces[0].shape
    depth = cache.shape[0]
    return pl.pallas_call(
        functools.partial(attend_kernel, count=count, scale=scale),
        out_shape=[jax.ShapeDtypeStruct((rows + TAIL, width), jnp.bfloat16)] * count,
        in_specs=[VMEM] * (count + 3),
        out_specs=[VMEM] * count,
        scratch_shapes=[
            pltpu.VMEM((rows, depth), jnp.bfloat16),
            pltpu.VMEM((rows, count * width), jnp.float32),
        ],
        compiler_params=pltpu.CompilerParams(vmem_limit_bytes=16 * MIB),
        name="attend",
    )(*pieces, rope, cache, bias)


def numbers_of(tail, rows):
    each = rows // LANES
    tail = tail.astype(jnp.float32)
    found = []
    for first in (0, 3 * each):
        parts = [
            jnp.concatenate([tail[at + i : at + i + 1] for i in range(each)], axis=1)
            for at in range(first, first + 3 * each, each)
        ]
        found.append(parts[0] + parts[1] + parts[2])
    return found


def values_kernel(*refs, drafts):
    blocks, value_absorb, out = refs[:-2], refs[-2], refs[-1]
    rows = out.shape[0]
    heads, width, value_width = value_absorb.shape
    numbers = [numbers_of(block[rows:, :], rows) for block in blocks]
    top = functools.reduce(jnp.maximum, [number[0] for number in numbers])
    factors = [jnp.exp(number[0] - top) for number in numbers]
    total = sum(factor * number[1] for factor, number in zip(factors, numbers))
    latent = jnp.zeros((rows, width), jnp.float32)
    for block, factor in zip(blocks, factors):
        column = jnp.broadcast_to(factor / total, (width, rows)).T
        latent += block[:rows, :].astype(jnp.float32) * column
    latent = latent.astype(jnp.bfloat16)
    pair = 2 * drafts
    first = lax.broadcasted_iota(jnp.int32, (pair, value_width), 0) < drafts
    for head in range(0, heads, 2):
        both = jnp.concatenate([value_absorb[head], value_absorb[head + 1]], axis=1)
        at = slice(head * drafts, head * drafts + pair)
        found = jnp.dot(latent[at], both, preferred_element_type=jnp.float32)
        out[at, :] = jnp.where(first, found[:, :value_width], found[:, value_width:]).astype(
            jnp.bfloat16
        )


def values_of(blocks, value_absorb, drafts):
    rows = blocks[0].shape[0] - TAIL
    return pl.pallas_call(
        functools.partial(values_kernel, drafts=drafts),
        out_shape=jax.ShapeDtypeStruct((rows, value_absorb.shape[2]), jnp.bfloat16),
        in_specs=[VMEM] * (len(blocks) + 1),
        out_specs=VMEM,
        compiler_params=pltpu.CompilerParams(vmem_limit_bytes=8 * MIB),
        name="values",
    )(*blocks, value_absorb)


def project_kernel(*refs, drafts):
    partials, weight, mine, theirs, flat, found = refs[:-5], *refs[-5:]
    rows, value_width = partials[0].shape
    summed = sum(partial[...].astype(jnp.float32) for partial in partials)
    for head in range(rows // drafts):
        flat[:, head * value_width : (head + 1) * value_width] = summed[
            head * drafts : (head + 1) * drafts
        ]
    found[...] = jnp.dot(
        flat[...].astype(jnp.bfloat16), weight[...], preferred_element_type=jnp.float32
    )
    half = mine.shape[1]
    me = lax.axis_index("head")
    mine[...] = found[:, pl.ds(pl.multiple_of(me * half, half), half)]
    theirs[...] = found[:, pl.ds(pl.multiple_of((1 - me) * half, half), half)]


def project(partials, weight, drafts):
    depth, width = weight.shape
    return pl.pallas_call(
        functools.partial(project_kernel, drafts=drafts),
        out_shape=[jax.ShapeDtypeStruct((drafts, width // 2), jnp.float32)] * 2,
        in_specs=[VMEM] * (len(partials) + 1),
        out_specs=[VMEM] * 2,
        scratch_shapes=[
            pltpu.VMEM((drafts, depth), jnp.float32),
            pltpu.VMEM((drafts, width), jnp.float32),
        ],
        compiler_params=pltpu.CompilerParams(vmem_limit_bytes=4 * MIB),
        name="project",
    )(*partials, weight)


def visibility(lengths, block_ids, tokens):
    drafts = block_ids.shape[1]
    first = lax.axis_index("ctx") * tokens
    position = first + jnp.arange(tokens, dtype=jnp.int32)
    blocks = first // BLK + jnp.arange(tokens // BLK, dtype=jnp.int32)
    chosen = jnp.any(block_ids[0][:, :, None] == blocks[None, None, :], axis=1)
    limit = lengths[0] - drafts + jnp.arange(drafts, dtype=jnp.int32)
    visible = jnp.repeat(chosen, BLK, axis=1) & (position[None, :] <= limit[:, None])
    bias = jnp.where(visible, 0.0, HIDDEN).astype(jnp.float32)
    return jnp.concatenate([bias] * (8 // drafts), axis=0)


def combine_many(block, rows):
    top, total = (line[0] for line in numbers_of(block[rows:, :LANES], rows))
    joint = lax.pmax(top, "ctx")
    factor = jnp.exp(top - joint)
    total = lax.psum(total * factor, "ctx")
    weighted = block[:rows].astype(jnp.float32) * factor[:, None]
    summed = lax.psum_scatter(weighted, "ctx", scatter_dimension=1, tiled=True)
    return (summed / total[:, None]).astype(jnp.bfloat16)


def local(
    query_nope,
    query_rope,
    latent_cache,
    lengths,
    block_ids,
    key_absorb,
    value_absorb,
    output_weight,
):
    _, drafts, heads, nope = query_nope.shape
    rope = query_rope.shape[3]
    tokens = latent_cache.shape[1]
    scale = (nope + rope) ** (-0.5)
    rows = drafts * heads
    peers = lax.axis_size("ctx")
    few = peers <= FEW and lax.axis_size("head") == 2 and key_absorb.shape[2] == LANES

    q_piece = jnp.einsum(
        "tho,hoc->htc", query_nope[0], key_absorb, preferred_element_type=jnp.float32
    ).astype(jnp.bfloat16)
    q_piece = q_piece.reshape(rows, -1)
    rope_rows = query_rope[0].transpose(1, 0, 2).reshape(rows, rope)
    bias = visibility(lengths, block_ids, tokens)
    cache = latent_cache[0].T
    if few:
        pieces = [q_piece] + [swap(q_piece, "ctx", step) for step in range(1, peers)]
        blocks = attend(pieces, rope_rows, cache, bias, scale)
        blocks = [blocks[0]] + [swap(blocks[step], "ctx", step) for step in range(1, peers)]
        partial = values_of(blocks, value_absorb, drafts)
        partials = [partial] + [swap(partial, "ctx", step) for step in range(1, peers)]
        mine, theirs = project(partials, output_weight, drafts)
        summed = mine + swap(theirs, "head", 1)
    else:
        queries = lax.all_gather(q_piece, "ctx", axis=1, tiled=True)
        block = attend([queries], rope_rows, cache, bias, scale)[0]
        o_latent = combine_many(block, rows)
        head_values = jnp.einsum(
            "htc,hcv->thv",
            o_latent.reshape(heads, drafts, -1),
            value_absorb,
            preferred_element_type=jnp.float32,
        )
        head_values = lax.psum(head_values, "ctx").astype(jnp.bfloat16)
        found = jnp.dot(
            head_values.reshape(drafts, -1), output_weight, preferred_element_type=jnp.float32
        )
        summed = lax.psum_scatter(found, "head", scatter_dimension=1, tiled=True)
    return summed.astype(jnp.bfloat16)[None]


def solution(mesh):
    placed = (
        P(("groups", "sub"), None, "head", None),
        P(("groups", "sub"), None, "head", None),
        P(("groups", "sub"), "ctx", None),
        P(("groups", "sub")),
        P(("groups", "sub"), None, None),
        P("head", None, "ctx"),
        P("head", "ctx", None),
        P("head", "ctx"),
    )
    return jax.shard_map(
        local,
        mesh=mesh,
        in_specs=placed,
        out_specs=P(("groups", "sub"), None, ("ctx", "head")),
        check_vma=False,
    )
```

```python
import functools

import jax
import jax.numpy as jnp
from jax import lax
from jax.experimental import pallas as pl
from jax.experimental.pallas import tpu as pltpu
from jax.sharding import PartitionSpec as P

BLK = 64
FEW = 4
LANES = 128
TAIL = 16
LOG2E = 1.4426950408889634
HIDDEN = -1e30
MIB = 1024 * 1024
VMEM = pl.BlockSpec(memory_space=pltpu.VMEM)
HBM = pl.BlockSpec(memory_space=pltpu.HBM)


def spans(microseconds):
    return pl.CostEstimate(flops=int(microseconds * 1e9), bytes_accessed=0, transcendentals=0)


def swap(value, axis, step):
    count = lax.axis_size(axis)
    return lax.ppermute(value, axis, [(i, i ^ step) for i in range(count)])


def thirds(value):
    high = value.astype(jnp.bfloat16)
    rest = value - high.astype(jnp.float32)
    middle = rest.astype(jnp.bfloat16)
    low = (rest - middle.astype(jnp.float32)).astype(jnp.bfloat16)
    return [part.astype(jnp.float32) for part in (high, middle, low)]


def by_head(value, rows_ref):
    drafts, heads, _ = value.shape
    for draft in range(drafts):
        rows_ref[pl.ds(draft, heads, stride=drafts), :] = value[draft].astype(jnp.float32)


def pair_products(left, heads, first, last, drafts, store):
    pair, width = 2 * drafts, heads.shape[2]
    upper = lax.broadcasted_iota(jnp.int32, (pair, width), 0) < drafts
    for head in range(first, last, 2):
        both = jnp.concatenate([heads[head], heads[head + 1]], axis=1)
        at = slice(head * drafts, head * drafts + pair)
        found = jnp.dot(left[at], both, preferred_element_type=jnp.float32)
        store[at, :] = jnp.where(upper, found[:, :width], found[:, width:]).astype(store.dtype)


def queries_kernel(query, key_absorb, out, query_here, held, rows_ref, arrived):
    drafts, heads, _ = query.shape
    parts = arrived.shape[0] - 1
    each = heads // parts
    copies = [pltpu.make_async_copy(query, query_here, arrived.at[parts])]
    for i in range(parts):
        at = pl.ds(i * each, each)
        copies.append(pltpu.make_async_copy(key_absorb.at[at], held.at[at], arrived.at[i]))
    for copy in copies:
        copy.start()
    copies[0].wait()
    by_head(query_here[...], rows_ref)
    left = rows_ref[...].astype(jnp.bfloat16)
    for i in range(parts):
        copies[1 + i].wait()
        pair_products(left, held, i * each, (i + 1) * each, drafts, out)


def queries_of(query, key_absorb):
    drafts, heads, nope = query.shape
    rows, width = drafts * heads, key_absorb.shape[2]
    return pl.pallas_call(
        queries_kernel,
        out_shape=pltpu.VMEM((rows, width), jnp.bfloat16),
        in_specs=[HBM] * 2,
        out_specs=VMEM,
        scratch_shapes=[
            pltpu.VMEM(query.shape, query.dtype),
            pltpu.VMEM(key_absorb.shape, key_absorb.dtype),
            pltpu.VMEM((rows, nope), jnp.float32),
            pltpu.SemaphoreType.DMA((min(4, heads // 2) + 1,)),
        ],
        compiler_params=pltpu.CompilerParams(vmem_limit_bytes=60 * MIB),
        name="queries",
    )(query, key_absorb)


def prepare_kernel(
    lengths, ids_there, rope_there, bias, rope_out, block_ids, query_rope, rows_ref, arrived
):
    drafts, chosen = block_ids.shape
    tokens = bias.shape[1]
    ids_copy = pltpu.make_async_copy(ids_there, block_ids, arrived.at[0])
    rope_copy = pltpu.make_async_copy(rope_there, query_rope, arrived.at[1])
    ids_copy.start()
    rope_copy.start()
    ids_copy.wait()
    ids = jnp.concatenate([block_ids[...]] * (8 // drafts), axis=0)
    position = lax.axis_index("ctx") * tokens + lax.broadcasted_iota(jnp.int32, (8, tokens), 1)
    block = position // BLK
    found = block == ids[:, :1]
    for i in range(1, chosen):
        found |= block == ids[:, i : i + 1]
    draft = lax.broadcasted_iota(jnp.int32, (8, tokens), 0) % drafts
    visible = found & (position <= lengths[0] - drafts + draft)
    bias[...] = jnp.where(visible, 0.0, HIDDEN)
    rope_copy.wait()
    by_head(query_rope[...], rows_ref)
    rope_out[...] = rows_ref[...].astype(jnp.bfloat16)


def prepare(lengths, block_ids, query_rope, tokens):
    drafts, heads, rope = query_rope.shape
    return pl.pallas_call(
        prepare_kernel,
        out_shape=[
            jax.ShapeDtypeStruct((8, tokens), jnp.float32),
            jax.ShapeDtypeStruct((drafts * heads, rope), jnp.bfloat16),
        ],
        in_specs=[pl.BlockSpec(memory_space=pltpu.SMEM), HBM, HBM],
        out_specs=[VMEM] * 2,
        scratch_shapes=[
            pltpu.VMEM(block_ids.shape, block_ids.dtype),
            pltpu.VMEM(query_rope.shape, query_rope.dtype),
            pltpu.VMEM((drafts * heads, rope), jnp.float32),
            pltpu.SemaphoreType.DMA((2,)),
        ],
        compiler_params=pltpu.CompilerParams(vmem_limit_bytes=4 * MIB),
        cost_estimate=spans(12),
        name="prepare",
    )(lengths, block_ids, query_rope)


def attend_kernel(*refs, count, scale):
    pieces, (rope, cache, bias) = refs[:count], refs[count : count + 3]
    outs, (queries, total_sums) = refs[count + 3 : -2], refs[-2:]
    rows, width = pieces[0].shape
    latent = count * width
    me = lax.axis_index("ctx") if count > 1 else 0
    for step in range(count):
        at = pl.multiple_of((me ^ step) * width, width)
        queries[:, pl.ds(at, width)] = pieces[step][...]
    queries[:, latent:] = rope[...]

    tokens = cache.shape[1]
    scores = jnp.dot(queries[...], cache[...], preferred_element_type=jnp.float32)
    scores = (scores.reshape(rows // 8, 8, tokens) + bias[...][None]).reshape(rows, tokens)
    top = jnp.max(scores, axis=1, keepdims=True)
    weights = jnp.exp2((scores - top) * (scale * LOG2E))
    total = jnp.sum(weights, axis=1, keepdims=True)
    total_sums[...] = lax.dot_general(
        weights.astype(jnp.bfloat16),
        cache[:latent, :],
        (((1,), (1,)), ((), ())),
        preferred_element_type=jnp.float32,
    )

    lines = []
    for value in (top * scale, total):
        line = jnp.broadcast_to(value, (rows, LANES)).T[:1]
        for part in thirds(line):
            lines += [part[:, at : at + LANES] for at in range(0, rows, LANES)]
    lines.append(jnp.zeros((TAIL - len(lines), LANES), jnp.float32))
    tail = jnp.concatenate(lines, axis=0).astype(jnp.bfloat16)
    for step in range(count):
        at = pl.multiple_of((me ^ step) * width, width)
        outs[step][:rows, :] = total_sums[:, pl.ds(at, width)].astype(jnp.bfloat16)
        outs[step][rows:, :LANES] = tail


def attend(pieces, rope, cache, bias, scale):
    count, (rows, width) = len(pieces), pieces[0].shape
    depth = cache.shape[0]
    return pl.pallas_call(
        functools.partial(attend_kernel, count=count, scale=scale),
        out_shape=[jax.ShapeDtypeStruct((rows + TAIL, width), jnp.bfloat16)] * count,
        in_specs=[VMEM] * (count + 3),
        out_specs=[VMEM] * count,
        scratch_shapes=[
            pltpu.VMEM((rows, depth), jnp.bfloat16),
            pltpu.VMEM((rows, count * width), jnp.float32),
        ],
        compiler_params=pltpu.CompilerParams(vmem_limit_bytes=16 * MIB),
        cost_estimate=spans(40),
        name="attend",
    )(*pieces, rope, cache, bias)


def numbers_of(tail, rows):
    each = rows // LANES
    tail = tail.astype(jnp.float32)
    found = []
    for first in (0, 3 * each):
        parts = [
            jnp.concatenate([tail[at + i : at + i + 1] for i in range(each)], axis=1)
            for at in range(first, first + 3 * each, each)
        ]
        found.append(parts[0] + parts[1] + parts[2])
    return found


def values_kernel(*refs, drafts):
    blocks, value_absorb, out = refs[:-2], refs[-2], refs[-1]
    rows = out.shape[0]
    heads, width, value_width = value_absorb.shape
    numbers = [numbers_of(block[rows:, :], rows) for block in blocks]
    top = functools.reduce(jnp.maximum, [number[0] for number in numbers])
    factors = [jnp.exp(number[0] - top) for number in numbers]
    total = sum(factor * number[1] for factor, number in zip(factors, numbers))
    latent = jnp.zeros((rows, width), jnp.float32)
    for block, factor in zip(blocks, factors):
        column = jnp.broadcast_to(factor / total, (width, rows)).T
        latent += block[:rows, :].astype(jnp.float32) * column
    latent = latent.astype(jnp.bfloat16)
    pair_products(latent, value_absorb, 0, heads, drafts, out)


def values_of(blocks, value_absorb, drafts):
    rows = blocks[0].shape[0] - TAIL
    return pl.pallas_call(
        functools.partial(values_kernel, drafts=drafts),
        out_shape=jax.ShapeDtypeStruct((rows, value_absorb.shape[2]), jnp.bfloat16),
        in_specs=[VMEM] * (len(blocks) + 1),
        out_specs=VMEM,
        compiler_params=pltpu.CompilerParams(vmem_limit_bytes=8 * MIB),
        name="values",
    )(*blocks, value_absorb)


def half_of(weight, other):
    half = weight.shape[1] // 2
    me = lax.axis_index("head")
    at = pl.multiple_of((1 - me if other else me) * half, half)
    return weight[:, pl.ds(at, half)]


def theirs_kernel(*refs, drafts):
    partials, (weight, theirs, flat, rows_ref) = refs[:-4], refs[-4:]
    rows, value_width = partials[0].shape
    summed = sum(partial[...].astype(jnp.float32) for partial in partials)
    for head in range(rows // drafts):
        rows_ref[:, head * value_width : (head + 1) * value_width] = summed[
            head * drafts : (head + 1) * drafts
        ]
    flat[...] = rows_ref[...].astype(jnp.bfloat16)
    theirs[...] = jnp.dot(flat[...], half_of(weight, True), preferred_element_type=jnp.float32)


def theirs_of(partials, weight, drafts):
    depth, width = weight.shape
    return pl.pallas_call(
        functools.partial(theirs_kernel, drafts=drafts),
        out_shape=[
            jax.ShapeDtypeStruct((drafts, width // 2), jnp.float32),
            jax.ShapeDtypeStruct((drafts, depth), jnp.bfloat16),
        ],
        in_specs=[VMEM] * (len(partials) + 1),
        out_specs=[VMEM] * 2,
        scratch_shapes=[pltpu.VMEM((drafts, depth), jnp.float32)],
        compiler_params=pltpu.CompilerParams(vmem_limit_bytes=4 * MIB),
        name="theirs",
    )(*partials, weight)


def mine_kernel(flat, weight, mine):
    mine[...] = jnp.dot(flat[...], half_of(weight, False), preferred_element_type=jnp.float32)


def mine_of(flat, weight):
    return pl.pallas_call(
        mine_kernel,
        out_shape=jax.ShapeDtypeStruct((flat.shape[0], weight.shape[1] // 2), jnp.float32),
        in_specs=[VMEM] * 2,
        out_specs=VMEM,
        compiler_params=pltpu.CompilerParams(vmem_limit_bytes=4 * MIB),
        cost_estimate=spans(2),
        name="mine",
    )(flat, weight)


def combine_many(block, rows):
    top, total = (line[0] for line in numbers_of(block[rows:, :LANES], rows))
    joint = lax.pmax(top, "ctx")
    factor = jnp.exp(top - joint)
    total = lax.psum(total * factor, "ctx")
    weighted = block[:rows].astype(jnp.float32) * factor[:, None]
    summed = lax.psum_scatter(weighted, "ctx", scatter_dimension=1, tiled=True)
    return (summed / total[:, None]).astype(jnp.bfloat16)


def local(
    query_nope,
    query_rope,
    latent_cache,
    lengths,
    block_ids,
    key_absorb,
    value_absorb,
    output_weight,
):
    _, drafts, heads, nope = query_nope.shape
    rope = query_rope.shape[3]
    tokens = latent_cache.shape[1]
    scale = (nope + rope) ** (-0.5)
    rows = drafts * heads
    peers = lax.axis_size("ctx")
    few = peers <= FEW and lax.axis_size("head") == 2 and key_absorb.shape[2] == LANES

    q_piece = queries_of(query_nope[0], key_absorb)
    bias, rope_rows = prepare(lengths, block_ids[0], query_rope[0], tokens)
    cache = latent_cache[0].T
    if few:
        pieces = [q_piece] + [swap(q_piece, "ctx", step) for step in range(1, peers)]
        blocks = attend(pieces, rope_rows, cache, bias, scale)
        blocks = [blocks[0]] + [swap(blocks[step], "ctx", step) for step in range(1, peers)]
        partial = values_of(blocks, value_absorb, drafts)
        partials = [partial] + [swap(partial, "ctx", step) for step in range(1, peers)]
        theirs, flat = theirs_of(partials, output_weight, drafts)
        summed = mine_of(flat, output_weight) + swap(theirs, "head", 1)
    else:
        queries = lax.all_gather(q_piece, "ctx", axis=1, tiled=True)
        block = attend([queries], rope_rows, cache, bias, scale)[0]
        o_latent = combine_many(block, rows)
        head_values = jnp.einsum(
            "htc,hcv->thv",
            o_latent.reshape(heads, drafts, -1),
            value_absorb,
            preferred_element_type=jnp.float32,
        )
        head_values = lax.psum(head_values, "ctx").astype(jnp.bfloat16)
        found = jnp.dot(
            head_values.reshape(drafts, -1), output_weight, preferred_element_type=jnp.float32
        )
        summed = lax.psum_scatter(found, "head", scatter_dimension=1, tiled=True)
    return summed.astype(jnp.bfloat16)[None]


def solution(mesh):
    placed = (
        P(("groups", "sub"), None, "head", None),
        P(("groups", "sub"), None, "head", None),
        P(("groups", "sub"), "ctx", None),
        P(("groups", "sub")),
        P(("groups", "sub"), None, None),
        P("head", None, "ctx"),
        P("head", "ctx", None),
        P("head", "ctx"),
    )
    return jax.shard_map(
        local,
        mesh=mesh,
        in_specs=placed,
        out_specs=P(("groups", "sub"), None, ("ctx", "head")),
        check_vma=False,
    )
```

```python
import functools

import jax
import jax.numpy as jnp
from jax import lax
from jax.experimental import pallas as pl
from jax.experimental.pallas import tpu as pltpu
from jax.sharding import PartitionSpec as P

BLK = 64
FEW = 4
LANES = 128
TAIL = 16
LOG2E = 1.4426950408889634
HIDDEN = -1e30
MIB = 1024 * 1024
VMEM = pl.BlockSpec(memory_space=pltpu.VMEM)
HBM = pl.BlockSpec(memory_space=pltpu.HBM)


def spans(microseconds):
    return pl.CostEstimate(flops=int(microseconds * 1e9), bytes_accessed=0, transcendentals=0)


def swap(value, axis, step):
    count = lax.axis_size(axis)
    return lax.ppermute(value, axis, [(i, i ^ step) for i in range(count)])


def thirds(value):
    high = value.astype(jnp.bfloat16)
    rest = value - high.astype(jnp.float32)
    middle = rest.astype(jnp.bfloat16)
    low = (rest - middle.astype(jnp.float32)).astype(jnp.bfloat16)
    return [part.astype(jnp.float32) for part in (high, middle, low)]


def by_head(value, rows_ref):
    drafts, heads, _ = value.shape
    for draft in range(drafts):
        rows_ref[pl.ds(draft, heads, stride=drafts), :] = value[draft].astype(jnp.float32)


def pair_products(left, heads, first, last, drafts, store):
    pair, width = 2 * drafts, heads.shape[2]
    upper = lax.broadcasted_iota(jnp.int32, (pair, width), 0) < drafts
    for head in range(first, last, 2):
        both = jnp.concatenate([heads[head], heads[head + 1]], axis=1)
        at = slice(head * drafts, head * drafts + pair)
        found = jnp.dot(left[at], both, preferred_element_type=jnp.float32)
        store[at, :] = jnp.where(upper, found[:, :width], found[:, width:]).astype(store.dtype)


def queries_kernel(query, key_absorb, out, query_here, held, rows_ref, arrived):
    drafts, heads, _ = query.shape
    parts = arrived.shape[0] - 1
    each = heads // parts
    copies = [pltpu.make_async_copy(query, query_here, arrived.at[parts])]
    for i in range(parts):
        at = pl.ds(i * each, each)
        copies.append(pltpu.make_async_copy(key_absorb.at[at], held.at[at], arrived.at[i]))
    for copy in copies:
        copy.start()
    copies[0].wait()
    by_head(query_here[...], rows_ref)
    left = rows_ref[...].astype(jnp.bfloat16)
    for i in range(parts):
        copies[1 + i].wait()
        pair_products(left, held, i * each, (i + 1) * each, drafts, out)


def queries_of(query, key_absorb):
    drafts, heads, nope = query.shape
    rows, width = drafts * heads, key_absorb.shape[2]
    return pl.pallas_call(
        queries_kernel,
        out_shape=pltpu.VMEM((rows, width), jnp.bfloat16),
        in_specs=[HBM] * 2,
        out_specs=VMEM,
        scratch_shapes=[
            pltpu.VMEM(query.shape, query.dtype),
            pltpu.VMEM(key_absorb.shape, key_absorb.dtype),
            pltpu.VMEM((rows, nope), jnp.float32),
            pltpu.SemaphoreType.DMA((min(4, heads // 2) + 1,)),
        ],
        compiler_params=pltpu.CompilerParams(vmem_limit_bytes=60 * MIB),
        cost_estimate=spans(5),
        name="queries",
    )(query, key_absorb)


def prepare_kernel(
    lengths, block_ids, query_rope, bias, rope_out, rows_ref
):
    drafts, chosen = block_ids.shape
    tokens = bias.shape[1]
    ids = jnp.concatenate([block_ids[...]] * (8 // drafts), axis=0)
    position = lax.axis_index("ctx") * tokens + lax.broadcasted_iota(jnp.int32, (8, tokens), 1)
    block = position // BLK
    found = block == ids[:, :1]
    for i in range(1, chosen):
        found |= block == ids[:, i : i + 1]
    draft = lax.broadcasted_iota(jnp.int32, (8, tokens), 0) % drafts
    visible = found & (position <= lengths[0] - drafts + draft)
    bias[...] = jnp.where(visible, 0.0, HIDDEN)
    by_head(query_rope[...], rows_ref)
    rope_out[...] = rows_ref[...].astype(jnp.bfloat16)


def prepare(lengths, block_ids, query_rope, tokens):
    drafts, heads, rope = query_rope.shape
    return pl.pallas_call(
        prepare_kernel,
        out_shape=[
            jax.ShapeDtypeStruct((8, tokens), jnp.float32),
            jax.ShapeDtypeStruct((drafts * heads, rope), jnp.bfloat16),
        ],
        in_specs=[pl.BlockSpec(memory_space=pltpu.SMEM), VMEM, VMEM],
        out_specs=[VMEM] * 2,
        scratch_shapes=[pltpu.VMEM((drafts * heads, rope), jnp.float32)],
        compiler_params=pltpu.CompilerParams(vmem_limit_bytes=4 * MIB),
        cost_estimate=spans(12),
        name="prepare",
    )(lengths, block_ids, query_rope)


def rows_at(ref, places, width):
    found = [ref[pl.ds(pl.multiple_of(place * width, width), width), :] for place in places]
    return found[0] if len(found) == 1 else jnp.concatenate(found, axis=0)


def slices_of(steps):
    return [lax.axis_index("ctx") ^ step for step in steps] if steps else [0]


def begin_kernel(*refs, steps):
    pieces, (rope, cache, bias, scores) = refs[:-4], refs[-4:]
    rows, width = pieces[0].shape
    depth, tokens = cache.shape
    found = jnp.dot(
        jnp.concatenate([piece[...] for piece in pieces], axis=1),
        rows_at(cache, slices_of(steps), width),
        preferred_element_type=jnp.float32,
    )
    found += jnp.dot(
        rope[...], cache[depth - rope.shape[1] :, :], preferred_element_type=jnp.float32
    )
    scores[...] = (found.reshape(rows // 8, 8, tokens) + bias[...][None]).reshape(rows, tokens)


def begin(pieces, steps, rope, cache, bias):
    rows, tokens = pieces[0].shape[0], cache.shape[1]
    return pl.pallas_call(
        functools.partial(begin_kernel, steps=steps),
        out_shape=jax.ShapeDtypeStruct((rows, tokens), jnp.float32),
        in_specs=[VMEM] * (len(pieces) + 3),
        out_specs=VMEM,
        compiler_params=pltpu.CompilerParams(vmem_limit_bytes=6 * MIB),
        name="begin",
    )(*pieces, rope, cache, bias)


def attend_kernel(*refs, steps, outs_of, scale):
    pieces, (begun, cache) = refs[: len(steps)], refs[len(steps) : len(steps) + 2]
    outs, total_sums = refs[len(steps) + 2 : -1], refs[-1]
    rows, latent = total_sums.shape
    width = latent // len(outs)
    scores = begun[...]
    if steps:
        scores += jnp.dot(
            jnp.concatenate([piece[...] for piece in pieces], axis=1),
            rows_at(cache, slices_of(steps), width),
            preferred_element_type=jnp.float32,
        )
    top = jnp.max(scores, axis=1, keepdims=True)
    weights = jnp.exp2((scores - top) * (scale * LOG2E))
    total = jnp.sum(weights, axis=1, keepdims=True)
    total_sums[...] = lax.dot_general(
        weights.astype(jnp.bfloat16),
        cache[:latent, :],
        (((1,), (1,)), ((), ())),
        preferred_element_type=jnp.float32,
    )

    lines = []
    for value in (top * scale, total):
        line = jnp.broadcast_to(value, (rows, LANES)).T[:1]
        for part in thirds(line):
            lines += [part[:, at : at + LANES] for at in range(0, rows, LANES)]
    lines.append(jnp.zeros((TAIL - len(lines), LANES), jnp.float32))
    tail = jnp.concatenate(lines, axis=0).astype(jnp.bfloat16)
    for out, place in zip(outs, slices_of(outs_of)):
        at = pl.multiple_of(place * width, width)
        out[:rows, :] = total_sums[:, pl.ds(at, width)].astype(jnp.bfloat16)
        out[rows:, :LANES] = tail


def attend(pieces, steps, begun, cache, latent, outs_of, scale):
    rows, count = begun.shape[0], max(len(outs_of), 1)
    return pl.pallas_call(
        functools.partial(attend_kernel, steps=steps, outs_of=outs_of, scale=scale),
        out_shape=[jax.ShapeDtypeStruct((rows + TAIL, latent // count), jnp.bfloat16)] * count,
        in_specs=[VMEM] * (len(pieces) + 2),
        out_specs=[VMEM] * count,
        scratch_shapes=[pltpu.VMEM((rows, latent), jnp.float32)],
        compiler_params=pltpu.CompilerParams(vmem_limit_bytes=11 * MIB),
        name="attend",
    )(*pieces, begun, cache)


def numbers_of(tail, rows):
    each = rows // LANES
    tail = tail.astype(jnp.float32)
    found = []
    for first in (0, 3 * each):
        parts = [
            jnp.concatenate([tail[at + i : at + i + 1] for i in range(each)], axis=1)
            for at in range(first, first + 3 * each, each)
        ]
        found.append(parts[0] + parts[1] + parts[2])
    return found


def keep_kernel(block, out):
    out[...] = block[...]


def keep(block):
    return pl.pallas_call(
        keep_kernel,
        out_shape=jax.ShapeDtypeStruct(block.shape, block.dtype),
        in_specs=[VMEM],
        out_specs=VMEM,
        compiler_params=pltpu.CompilerParams(vmem_limit_bytes=1 * MIB),
        cost_estimate=spans(40),
        name="keep",
    )(block)


def values_kernel(*refs, drafts):
    blocks, value_absorb, out = refs[:-2], refs[-2], refs[-1]
    rows = out.shape[0]
    heads, width, value_width = value_absorb.shape
    numbers = [numbers_of(block[rows:, :], rows) for block in blocks]
    top = functools.reduce(jnp.maximum, [number[0] for number in numbers])
    factors = [jnp.exp(number[0] - top) for number in numbers]
    total = sum(factor * number[1] for factor, number in zip(factors, numbers))
    latent = jnp.zeros((rows, width), jnp.float32)
    for block, factor in zip(blocks, factors):
        column = jnp.broadcast_to(factor / total, (width, rows)).T
        latent += block[:rows, :].astype(jnp.float32) * column
    latent = latent.astype(jnp.bfloat16)
    pair_products(latent, value_absorb, 0, heads, drafts, out)


def values_of(blocks, value_absorb, drafts):
    rows = blocks[0].shape[0] - TAIL
    return pl.pallas_call(
        functools.partial(values_kernel, drafts=drafts),
        out_shape=jax.ShapeDtypeStruct((rows, value_absorb.shape[2]), jnp.bfloat16),
        in_specs=[VMEM] * (len(blocks) + 1),
        out_specs=VMEM,
        compiler_params=pltpu.CompilerParams(vmem_limit_bytes=8 * MIB),
        name="values",
    )(*blocks, value_absorb)


def half_of(weight, other):
    half = weight.shape[1] // 2
    me = lax.axis_index("head")
    at = pl.multiple_of((1 - me if other else me) * half, half)
    return weight[:, pl.ds(at, half)]


def theirs_kernel(*refs, drafts):
    partials, (weight, theirs, flat, rows_ref) = refs[:-4], refs[-4:]
    rows, value_width = partials[0].shape
    summed = sum(partial[...].astype(jnp.float32) for partial in partials)
    for head in range(rows // drafts):
        rows_ref[:, head * value_width : (head + 1) * value_width] = summed[
            head * drafts : (head + 1) * drafts
        ]
    flat[...] = rows_ref[...].astype(jnp.bfloat16)
    theirs[...] = jnp.dot(flat[...], half_of(weight, True), preferred_element_type=jnp.float32)


def theirs_of(partials, weight, drafts):
    depth, width = weight.shape
    return pl.pallas_call(
        functools.partial(theirs_kernel, drafts=drafts),
        out_shape=[
            jax.ShapeDtypeStruct((drafts, width // 2), jnp.float32),
            jax.ShapeDtypeStruct((drafts, depth), jnp.bfloat16),
        ],
        in_specs=[VMEM] * (len(partials) + 1),
        out_specs=[VMEM] * 2,
        scratch_shapes=[pltpu.VMEM((drafts, depth), jnp.float32)],
        compiler_params=pltpu.CompilerParams(vmem_limit_bytes=4 * MIB),
        name="theirs",
    )(*partials, weight)


def mine_kernel(flat, weight, mine):
    mine[...] = jnp.dot(flat[...], half_of(weight, False), preferred_element_type=jnp.float32)


def mine_of(flat, weight):
    return pl.pallas_call(
        mine_kernel,
        out_shape=jax.ShapeDtypeStruct((flat.shape[0], weight.shape[1] // 2), jnp.float32),
        in_specs=[VMEM] * 2,
        out_specs=VMEM,
        compiler_params=pltpu.CompilerParams(vmem_limit_bytes=4 * MIB),
        cost_estimate=spans(2),
        name="mine",
    )(flat, weight)


def combine_many(block, rows):
    top, total = (line[0] for line in numbers_of(block[rows:, :LANES], rows))
    joint = lax.pmax(top, "ctx")
    factor = jnp.exp(top - joint)
    total = lax.psum(total * factor, "ctx")
    weighted = block[:rows].astype(jnp.float32) * factor[:, None]
    summed = lax.psum_scatter(weighted, "ctx", scatter_dimension=1, tiled=True)
    return (summed / total[:, None]).astype(jnp.bfloat16)


def local(
    query_nope,
    query_rope,
    latent_cache,
    lengths,
    block_ids,
    key_absorb,
    value_absorb,
    output_weight,
):
    _, drafts, heads, nope = query_nope.shape
    rope = query_rope.shape[3]
    tokens = latent_cache.shape[1]
    scale = (nope + rope) ** (-0.5)
    rows, latent = drafts * heads, latent_cache.shape[2] - rope
    peers = lax.axis_size("ctx")
    few = peers <= FEW and lax.axis_size("head") == 2 and key_absorb.shape[2] == LANES

    q_piece = queries_of(query_nope[0], key_absorb)
    bias, rope_rows = prepare(lengths, block_ids[0], query_rope[0], tokens)
    cache = latent_cache[0].T
    if few:
        steps = tuple(range(peers))
        pieces = [q_piece] + [swap(q_piece, "ctx", step) for step in steps[1:]]
        early, late = (0, 1), (2, 3)
        begun = begin([pieces[step] for step in early], early, rope_rows, cache, bias)
        blocks = attend(
            [pieces[step] for step in late], late, begun, cache, latent, steps, scale
        )
        blocks = [keep(blocks[0])] + [swap(blocks[step], "ctx", step) for step in (2, 3, 1)]
        partial = values_of(blocks, value_absorb, drafts)
        partials = [partial] + [swap(partial, "ctx", step) for step in (2, 3, 1)]
        theirs, flat = theirs_of(partials, output_weight, drafts)
        summed = mine_of(flat, output_weight) + swap(theirs, "head", 1)
    else:
        queries = lax.all_gather(q_piece, "ctx", axis=1, tiled=True)
        begun = begin([queries], (), rope_rows, cache, bias)
        block = attend([], (), begun, cache, latent, (), scale)[0]
        o_latent = combine_many(block, rows)
        head_values = jnp.einsum(
            "htc,hcv->thv",
            o_latent.reshape(heads, drafts, -1),
            value_absorb,
            preferred_element_type=jnp.float32,
        )
        head_values = lax.psum(head_values, "ctx").astype(jnp.bfloat16)
        found = jnp.dot(
            head_values.reshape(drafts, -1), output_weight, preferred_element_type=jnp.float32
        )
        summed = lax.psum_scatter(found, "head", scatter_dimension=1, tiled=True)
    return summed.astype(jnp.bfloat16)[None]


def solution(mesh):
    placed = (
        P(("groups", "sub"), None, "head", None),
        P(("groups", "sub"), None, "head", None),
        P(("groups", "sub"), "ctx", None),
        P(("groups", "sub")),
        P(("groups", "sub"), None, None),
        P("head", None, "ctx"),
        P("head", "ctx", None),
        P("head", "ctx"),
    )
    return jax.shard_map(
        local,
        mesh=mesh,
        in_specs=placed,
        out_specs=P(("groups", "sub"), None, ("ctx", "head")),
        check_vma=False,
    )
```

```python
import functools

import jax
import jax.numpy as jnp
from jax import lax
from jax.experimental import pallas as pl
from jax.experimental.pallas import tpu as pltpu
from jax.sharding import PartitionSpec as P

BLK = 64
FEW = 4
LANES = 128
TAIL = 16
LOG2E = 1.4426950408889634
HIDDEN = -1e30
MIB = 1024 * 1024
VMEM = pl.BlockSpec(memory_space=pltpu.VMEM)
HBM = pl.BlockSpec(memory_space=pltpu.HBM)


def spans(microseconds):
    return pl.CostEstimate(flops=int(microseconds * 1e9), bytes_accessed=0, transcendentals=0)


def swap(value, axis, step):
    count = lax.axis_size(axis)
    return lax.ppermute(value, axis, [(i, i ^ step) for i in range(count)])


def thirds(value):
    high = value.astype(jnp.bfloat16)
    rest = value - high.astype(jnp.float32)
    middle = rest.astype(jnp.bfloat16)
    low = (rest - middle.astype(jnp.float32)).astype(jnp.bfloat16)
    return [part.astype(jnp.float32) for part in (high, middle, low)]


def by_head(value, rows_ref):
    drafts, heads, _ = value.shape
    for draft in range(drafts):
        rows_ref[pl.ds(draft, heads, stride=drafts), :] = value[draft].astype(jnp.float32)


def pair_products(left, heads, first, last, drafts, store):
    pair, width = 2 * drafts, heads.shape[2]
    upper = lax.broadcasted_iota(jnp.int32, (pair, width), 0) < drafts
    for head in range(first, last, 2):
        both = jnp.concatenate([heads[head], heads[head + 1]], axis=1)
        at = slice(head * drafts, head * drafts + pair)
        found = jnp.dot(
            left[at].astype(jnp.bfloat16), both, preferred_element_type=jnp.float32
        )
        store[at, :] = jnp.where(upper, found[:, :width], found[:, width:])


def queries_kernel(query, key_absorb, out, query_here, held, rows_ref, found, arrived):
    drafts, heads, _ = query.shape
    parts = arrived.shape[0] - 1
    each = heads // parts
    copies = [pltpu.make_async_copy(query, query_here, arrived.at[parts])]
    for i in range(parts):
        at = pl.ds(i * each, each)
        copies.append(pltpu.make_async_copy(key_absorb.at[at], held.at[at], arrived.at[i]))
    for copy in copies:
        copy.start()
    copies[0].wait()
    by_head(query_here[...], rows_ref)
    left = rows_ref[...]
    for i in range(parts):
        copies[1 + i].wait()
        pair_products(left, held, i * each, (i + 1) * each, drafts, found)
    out[...] = found[...].astype(out.dtype)


def queries_of(query, key_absorb):
    drafts, heads, nope = query.shape
    rows, width = drafts * heads, key_absorb.shape[2]
    return pl.pallas_call(
        queries_kernel,
        out_shape=pltpu.VMEM((rows, width), jnp.bfloat16),
        in_specs=[HBM] * 2,
        out_specs=VMEM,
        scratch_shapes=[
            pltpu.VMEM(query.shape, query.dtype),
            pltpu.VMEM(key_absorb.shape, key_absorb.dtype),
            pltpu.VMEM((rows, nope), jnp.float32),
            pltpu.VMEM((rows, width), jnp.float32),
            pltpu.SemaphoreType.DMA((min(4, heads // 2) + 1,)),
        ],
        compiler_params=pltpu.CompilerParams(vmem_limit_bytes=60 * MIB),
        cost_estimate=spans(5),
        name="queries",
    )(query, key_absorb)


def prepare_kernel(
    lengths, block_ids, query_rope, bias, rope_out, rows_ref
):
    drafts, chosen = block_ids.shape
    tokens = bias.shape[1]
    ids = jnp.concatenate([block_ids[...]] * (8 // drafts), axis=0)
    position = lax.axis_index("ctx") * tokens + lax.broadcasted_iota(jnp.int32, (8, tokens), 1)
    block = position // BLK
    found = block == ids[:, :1]
    for i in range(1, chosen):
        found |= block == ids[:, i : i + 1]
    draft = lax.broadcasted_iota(jnp.int32, (8, tokens), 0) % drafts
    visible = found & (position <= lengths[0] - drafts + draft)
    bias[...] = jnp.where(visible, 0.0, HIDDEN)
    by_head(query_rope[...], rows_ref)
    rope_out[...] = rows_ref[...].astype(jnp.bfloat16)


def prepare(lengths, block_ids, query_rope, tokens):
    drafts, heads, rope = query_rope.shape
    return pl.pallas_call(
        prepare_kernel,
        out_shape=[
            jax.ShapeDtypeStruct((8, tokens), jnp.float32),
            jax.ShapeDtypeStruct((drafts * heads, rope), jnp.bfloat16),
        ],
        in_specs=[pl.BlockSpec(memory_space=pltpu.SMEM), VMEM, VMEM],
        out_specs=[VMEM] * 2,
        scratch_shapes=[pltpu.VMEM((drafts * heads, rope), jnp.float32)],
        compiler_params=pltpu.CompilerParams(vmem_limit_bytes=4 * MIB),
        cost_estimate=spans(12),
        name="prepare",
    )(lengths, block_ids, query_rope)


def rows_at(ref, places, width):
    found = [ref[pl.ds(pl.multiple_of(place * width, width), width), :] for place in places]
    return found[0] if len(found) == 1 else jnp.concatenate(found, axis=0)


def slices_of(steps):
    return [lax.axis_index("ctx") ^ step for step in steps] if steps else [0]


def begin_kernel(*refs, steps):
    pieces, (rope, cache, bias, scores) = refs[:-4], refs[-4:]
    rows, width = pieces[0].shape
    depth, tokens = cache.shape
    found = jnp.dot(
        jnp.concatenate([piece[...] for piece in pieces], axis=1),
        rows_at(cache, slices_of(steps), width),
        preferred_element_type=jnp.float32,
    )
    found += jnp.dot(
        rope[...], cache[depth - rope.shape[1] :, :], preferred_element_type=jnp.float32
    )
    scores[...] = (found.reshape(rows // 8, 8, tokens) + bias[...][None]).reshape(rows, tokens)


def begin(pieces, steps, rope, cache, bias):
    rows, tokens = pieces[0].shape[0], cache.shape[1]
    return pl.pallas_call(
        functools.partial(begin_kernel, steps=steps),
        out_shape=jax.ShapeDtypeStruct((rows, tokens), jnp.float32),
        in_specs=[VMEM] * (len(pieces) + 3),
        out_specs=VMEM,
        compiler_params=pltpu.CompilerParams(vmem_limit_bytes=6 * MIB),
        name="begin",
    )(*pieces, rope, cache, bias)


def attend_kernel(*refs, steps, outs_of, scale):
    pieces, (begun, cache) = refs[: len(steps)], refs[len(steps) : len(steps) + 2]
    outs, total_sums = refs[len(steps) + 2 : -1], refs[-1]
    rows, latent = total_sums.shape
    width = latent // len(outs)
    scores = begun[...]
    if steps:
        scores += jnp.dot(
            jnp.concatenate([piece[...] for piece in pieces], axis=1),
            rows_at(cache, slices_of(steps), width),
            preferred_element_type=jnp.float32,
        )
    top = jnp.max(scores, axis=1, keepdims=True)
    weights = jnp.exp2((scores - top) * (scale * LOG2E))
    total = jnp.sum(weights, axis=1, keepdims=True)
    total_sums[...] = lax.dot_general(
        weights.astype(jnp.bfloat16),
        cache[:latent, :],
        (((1,), (1,)), ((), ())),
        preferred_element_type=jnp.float32,
    )

    lines = []
    for value in (top * scale, total):
        line = jnp.broadcast_to(value, (rows, LANES)).T[:1]
        for part in thirds(line):
            lines += [part[:, at : at + LANES] for at in range(0, rows, LANES)]
    lines.append(jnp.zeros((TAIL - len(lines), LANES), jnp.float32))
    tail = jnp.concatenate(lines, axis=0).astype(jnp.bfloat16)
    for out, place in zip(outs, slices_of(outs_of)):
        at = pl.multiple_of(place * width, width)
        out[:rows, :] = total_sums[:, pl.ds(at, width)].astype(jnp.bfloat16)
        out[rows:, :LANES] = tail


def attend(pieces, steps, begun, cache, latent, outs_of, scale):
    rows, count = begun.shape[0], max(len(outs_of), 1)
    return pl.pallas_call(
        functools.partial(attend_kernel, steps=steps, outs_of=outs_of, scale=scale),
        out_shape=[jax.ShapeDtypeStruct((rows + TAIL, latent // count), jnp.bfloat16)] * count,
        in_specs=[VMEM] * (len(pieces) + 2),
        out_specs=[VMEM] * count,
        scratch_shapes=[pltpu.VMEM((rows, latent), jnp.float32)],
        compiler_params=pltpu.CompilerParams(vmem_limit_bytes=11 * MIB),
        name="attend",
    )(*pieces, begun, cache)


def numbers_of(tail, rows):
    each = rows // LANES
    tail = tail.astype(jnp.float32)
    found = []
    for first in (0, 3 * each):
        parts = [
            jnp.concatenate([tail[at + i : at + i + 1] for i in range(each)], axis=1)
            for at in range(first, first + 3 * each, each)
        ]
        found.append(parts[0] + parts[1] + parts[2])
    return found


def keep_kernel(block, out):
    out[...] = block[...]


def keep(block):
    return pl.pallas_call(
        keep_kernel,
        out_shape=jax.ShapeDtypeStruct(block.shape, block.dtype),
        in_specs=[VMEM],
        out_specs=VMEM,
        compiler_params=pltpu.CompilerParams(vmem_limit_bytes=1 * MIB),
        cost_estimate=spans(40),
        name="keep",
    )(block)


def values_kernel(*refs, drafts):
    blocks, (value_absorb, out, found) = refs[:-3], refs[-3:]
    rows = out.shape[0]
    heads, width, value_width = value_absorb.shape
    numbers = [numbers_of(block[rows:, :], rows) for block in blocks]
    top = functools.reduce(jnp.maximum, [number[0] for number in numbers])
    factors = [jnp.exp(number[0] - top) for number in numbers]
    total = sum(factor * number[1] for factor, number in zip(factors, numbers))
    latent = jnp.zeros((rows, width), jnp.float32)
    for block, factor in zip(blocks, factors):
        column = jnp.broadcast_to(factor / total, (width, rows)).T
        latent += block[:rows, :].astype(jnp.float32) * column
    pair_products(latent, value_absorb, 0, heads, drafts, found)
    out[...] = found[...].astype(out.dtype)


def values_of(blocks, value_absorb, drafts):
    rows = blocks[0].shape[0] - TAIL
    return pl.pallas_call(
        functools.partial(values_kernel, drafts=drafts),
        out_shape=jax.ShapeDtypeStruct((rows, value_absorb.shape[2]), jnp.bfloat16),
        in_specs=[VMEM] * (len(blocks) + 1),
        out_specs=VMEM,
        scratch_shapes=[pltpu.VMEM((rows, value_absorb.shape[2]), jnp.float32)],
        compiler_params=pltpu.CompilerParams(vmem_limit_bytes=8 * MIB),
        name="values",
    )(*blocks, value_absorb)


def half_of(weight, other):
    half = weight.shape[1] // 2
    me = lax.axis_index("head")
    at = pl.multiple_of((1 - me if other else me) * half, half)
    return weight[:, pl.ds(at, half)]


def theirs_kernel(*refs, drafts):
    partials, (weight, theirs, flat, rows_ref) = refs[:-4], refs[-4:]
    rows, value_width = partials[0].shape
    summed = sum(partial[...].astype(jnp.float32) for partial in partials)
    for head in range(rows // drafts):
        rows_ref[:, head * value_width : (head + 1) * value_width] = summed[
            head * drafts : (head + 1) * drafts
        ]
    flat[...] = rows_ref[...].astype(jnp.bfloat16)
    theirs[...] = jnp.dot(flat[...], half_of(weight, True), preferred_element_type=jnp.float32)


def theirs_of(partials, weight, drafts):
    depth, width = weight.shape
    return pl.pallas_call(
        functools.partial(theirs_kernel, drafts=drafts),
        out_shape=[
            jax.ShapeDtypeStruct((drafts, width // 2), jnp.float32),
            jax.ShapeDtypeStruct((drafts, depth), jnp.bfloat16),
        ],
        in_specs=[VMEM] * (len(partials) + 1),
        out_specs=[VMEM] * 2,
        scratch_shapes=[pltpu.VMEM((drafts, depth), jnp.float32)],
        compiler_params=pltpu.CompilerParams(vmem_limit_bytes=4 * MIB),
        name="theirs",
    )(*partials, weight)


def mine_kernel(flat, weight, mine):
    mine[...] = jnp.dot(flat[...], half_of(weight, False), preferred_element_type=jnp.float32)


def mine_of(flat, weight):
    return pl.pallas_call(
        mine_kernel,
        out_shape=jax.ShapeDtypeStruct((flat.shape[0], weight.shape[1] // 2), jnp.float32),
        in_specs=[VMEM] * 2,
        out_specs=VMEM,
        compiler_params=pltpu.CompilerParams(vmem_limit_bytes=4 * MIB),
        cost_estimate=spans(2),
        name="mine",
    )(flat, weight)


def combine_many(block, rows):
    top, total = (line[0] for line in numbers_of(block[rows:, :LANES], rows))
    joint = lax.pmax(top, "ctx")
    factor = jnp.exp(top - joint)
    total = lax.psum(total * factor, "ctx")
    weighted = block[:rows].astype(jnp.float32) * factor[:, None]
    summed = lax.psum_scatter(weighted, "ctx", scatter_dimension=1, tiled=True)
    return (summed / total[:, None]).astype(jnp.bfloat16)


def local(
    query_nope,
    query_rope,
    latent_cache,
    lengths,
    block_ids,
    key_absorb,
    value_absorb,
    output_weight,
):
    _, drafts, heads, nope = query_nope.shape
    rope = query_rope.shape[3]
    tokens = latent_cache.shape[1]
    scale = (nope + rope) ** (-0.5)
    rows, latent = drafts * heads, latent_cache.shape[2] - rope
    peers = lax.axis_size("ctx")
    few = peers <= FEW and lax.axis_size("head") == 2 and key_absorb.shape[2] == LANES

    q_piece = queries_of(query_nope[0], key_absorb)
    bias, rope_rows = prepare(lengths, block_ids[0], query_rope[0], tokens)
    cache = latent_cache[0].T
    if few:
        steps = tuple(range(peers))
        pieces = [q_piece] + [swap(q_piece, "ctx", step) for step in steps[1:]]
        early, late = (0, 1), (2, 3)
        begun = begin([pieces[step] for step in early], early, rope_rows, cache, bias)
        blocks = attend(
            [pieces[step] for step in late], late, begun, cache, latent, steps, scale
        )
        blocks = [keep(blocks[0])] + [swap(blocks[step], "ctx", step) for step in (2, 3, 1)]
        partial = values_of(blocks, value_absorb, drafts)
        partials = [partial] + [swap(partial, "ctx", step) for step in (2, 3, 1)]
        theirs, flat = theirs_of(partials, output_weight, drafts)
        summed = mine_of(flat, output_weight) + swap(theirs, "head", 1)
    else:
        queries = lax.all_gather(q_piece, "ctx", axis=1, tiled=True)
        begun = begin([queries], (), rope_rows, cache, bias)
        block = attend([], (), begun, cache, latent, (), scale)[0]
        o_latent = combine_many(block, rows)
        head_values = jnp.einsum(
            "htc,hcv->thv",
            o_latent.reshape(heads, drafts, -1),
            value_absorb,
            preferred_element_type=jnp.float32,
        )
        head_values = lax.psum(head_values, "ctx").astype(jnp.bfloat16)
        found = jnp.dot(
            head_values.reshape(drafts, -1), output_weight, preferred_element_type=jnp.float32
        )
        summed = lax.psum_scatter(found, "head", scatter_dimension=1, tiled=True)
    return summed.astype(jnp.bfloat16)[None]


def solution(mesh):
    placed = (
        P(("groups", "sub"), None, "head", None),
        P(("groups", "sub"), None, "head", None),
        P(("groups", "sub"), "ctx", None),
        P(("groups", "sub")),
        P(("groups", "sub"), None, None),
        P("head", None, "ctx"),
        P("head", "ctx", None),
        P("head", "ctx"),
    )
    return jax.shard_map(
        local,
        mesh=mesh,
        in_specs=placed,
        out_specs=P(("groups", "sub"), None, ("ctx", "head")),
        check_vma=False,
    )
```

```python
import functools

import jax
import jax.numpy as jnp
from jax import lax
from jax.experimental import pallas as pl
from jax.experimental.pallas import tpu as pltpu
from jax.sharding import PartitionSpec as P

BLK = 64
PEERS = 4
LANES = 128
CHUNK = 512
TAIL = 16
LOG2E = 1.4426950408889634
HIDDEN = -1e30
MIB = 1024 * 1024
VMEM = pl.BlockSpec(memory_space=pltpu.VMEM)
HBM = pl.BlockSpec(memory_space=pltpu.HBM)


def spans(microseconds):
    return pl.CostEstimate(flops=int(microseconds * 1e9), bytes_accessed=0, transcendentals=0)


def swap(value, axis, step):
    count = lax.axis_size(axis)
    return lax.ppermute(value, axis, [(i, i ^ step) for i in range(count)])


def turn(value, axis, step):
    order = (0, 1, 3, 2)
    return lax.ppermute(value, axis, [(order[i], order[(i + step) % 4]) for i in range(4)])


def thirds(value):
    high = value.astype(jnp.bfloat16)
    rest = value - high.astype(jnp.float32)
    middle = rest.astype(jnp.bfloat16)
    low = (rest - middle.astype(jnp.float32)).astype(jnp.bfloat16)
    return [part.astype(jnp.float32) for part in (high, middle, low)]


def by_head(value, rows_ref):
    drafts, heads, _ = value.shape
    for draft in range(drafts):
        rows_ref[pl.ds(draft, heads, stride=drafts), :] = value[draft].astype(jnp.float32)


def pair_products(left, heads, first, last, drafts, store):
    pair, width = 2 * drafts, heads.shape[2]
    upper = lax.broadcasted_iota(jnp.int32, (pair, width), 0) < drafts
    for head in range(first, last, 2):
        both = jnp.concatenate([heads[head], heads[head + 1]], axis=1)
        at = slice(head * drafts, head * drafts + pair)
        found = jnp.dot(
            left[at].astype(jnp.bfloat16), both, preferred_element_type=jnp.float32
        )
        store[at, :] = jnp.where(upper, found[:, :width], found[:, width:])


def queries_kernel(query, key_absorb, out, query_here, held, rows_ref, found, arrived):
    drafts, heads, _ = query.shape
    parts = arrived.shape[0] - 1
    each = heads // parts
    copies = [pltpu.make_async_copy(query, query_here, arrived.at[parts])]
    for i in range(parts):
        at = pl.ds(i * each, each)
        copies.append(pltpu.make_async_copy(key_absorb.at[at], held.at[at], arrived.at[i]))
    for copy in copies:
        copy.start()
    copies[0].wait()
    by_head(query_here[...], rows_ref)
    left = rows_ref[...]
    for i in range(parts):
        copies[1 + i].wait()
        pair_products(left, held, i * each, (i + 1) * each, drafts, found)
    out[...] = found[...].astype(out.dtype)


def queries_of(query, key_absorb):
    drafts, heads, nope = query.shape
    rows, width = drafts * heads, key_absorb.shape[2]
    return pl.pallas_call(
        queries_kernel,
        out_shape=pltpu.VMEM((rows, width), jnp.bfloat16),
        in_specs=[HBM] * 2,
        out_specs=VMEM,
        scratch_shapes=[
            pltpu.VMEM(query.shape, query.dtype),
            pltpu.VMEM(key_absorb.shape, key_absorb.dtype),
            pltpu.VMEM((rows, nope), jnp.float32),
            pltpu.VMEM((rows, width), jnp.float32),
            pltpu.SemaphoreType.DMA((min(4, heads // 2) + 1,)),
        ],
        compiler_params=pltpu.CompilerParams(vmem_limit_bytes=60 * MIB),
        cost_estimate=spans(5),
        name="queries",
    )(query, key_absorb)


def prepare_kernel(
    lengths, block_ids, query_rope, bias, rope_out, rows_ref
):
    drafts, chosen = block_ids.shape
    tokens = bias.shape[1]
    ids = jnp.concatenate([block_ids[...]] * (8 // drafts), axis=0)
    position = lax.axis_index("ctx") * tokens + lax.broadcasted_iota(jnp.int32, (8, tokens), 1)
    block = position // BLK
    found = block == ids[:, :1]
    for i in range(1, chosen):
        found |= block == ids[:, i : i + 1]
    draft = lax.broadcasted_iota(jnp.int32, (8, tokens), 0) % drafts
    visible = found & (position <= lengths[0] - drafts + draft)
    bias[...] = jnp.where(visible, 0.0, HIDDEN)
    by_head(query_rope[...], rows_ref)
    rope_out[...] = rows_ref[...].astype(jnp.bfloat16)


def prepare(lengths, block_ids, query_rope, tokens):
    drafts, heads, rope = query_rope.shape
    return pl.pallas_call(
        prepare_kernel,
        out_shape=[
            jax.ShapeDtypeStruct((8, tokens), jnp.float32),
            jax.ShapeDtypeStruct((drafts * heads, rope), jnp.bfloat16),
        ],
        in_specs=[pl.BlockSpec(memory_space=pltpu.SMEM), VMEM, VMEM],
        out_specs=[VMEM] * 2,
        scratch_shapes=[pltpu.VMEM((drafts * heads, rope), jnp.float32)],
        compiler_params=pltpu.CompilerParams(vmem_limit_bytes=4 * MIB),
        cost_estimate=spans(12),
        name="prepare",
    )(lengths, block_ids, query_rope)


def rows_at(ref, places, width):
    found = [ref[pl.ds(pl.multiple_of(place * width, width), width), :] for place in places]
    return found[0] if len(found) == 1 else jnp.concatenate(found, axis=0)


def slices_of(steps):
    return [lax.axis_index("ctx") ^ step for step in steps] if steps else [0]


def begin_kernel(*refs, steps):
    pieces, (rope, cache, bias, scores) = refs[:-4], refs[-4:]
    rows, width = pieces[0].shape
    depth, tokens = cache.shape
    found = jnp.dot(
        jnp.concatenate([piece[...] for piece in pieces], axis=1),
        rows_at(cache, slices_of(steps), width),
        preferred_element_type=jnp.float32,
    )
    found += jnp.dot(
        rope[...], cache[depth - rope.shape[1] :, :], preferred_element_type=jnp.float32
    )
    scores[...] = (found.reshape(rows // 8, 8, tokens) + bias[...][None]).reshape(rows, tokens)


def begin(pieces, steps, rope, cache, bias):
    rows, tokens = pieces[0].shape[0], cache.shape[1]
    return pl.pallas_call(
        functools.partial(begin_kernel, steps=steps),
        out_shape=jax.ShapeDtypeStruct((rows, tokens), jnp.float32),
        in_specs=[VMEM] * (len(pieces) + 3),
        out_specs=VMEM,
        compiler_params=pltpu.CompilerParams(vmem_limit_bytes=6 * MIB),
        name="begin",
    )(*pieces, rope, cache, bias)


def attend_kernel(*refs, steps, outs_of, scale):
    pieces, (begun, cache) = refs[: len(steps)], refs[len(steps) : len(steps) + 2]
    outs, total_sums = refs[len(steps) + 2 : -1], refs[-1]
    rows, latent = total_sums.shape
    width = latent // len(outs)
    scores = begun[...]
    if steps:
        scores += jnp.dot(
            jnp.concatenate([piece[...] for piece in pieces], axis=1),
            rows_at(cache, slices_of(steps), width),
            preferred_element_type=jnp.float32,
        )
    top = jnp.max(scores, axis=1, keepdims=True)
    tokens = scores.shape[1]
    total = jnp.zeros((rows, 1), jnp.float32)
    sums = jnp.zeros((rows, latent), jnp.float32)
    for first in range(0, tokens, CHUNK):
        at = slice(first, first + CHUNK)
        weights = jnp.exp2((scores[:, at] - top) * (scale * LOG2E))
        total += jnp.sum(weights, axis=1, keepdims=True)
        sums += lax.dot_general(
            weights.astype(jnp.bfloat16),
            cache[:latent, at],
            (((1,), (1,)), ((), ())),
            preferred_element_type=jnp.float32,
        )
    total_sums[...] = sums

    lines = []
    for value in (top * scale, total):
        line = jnp.broadcast_to(value, (rows, LANES)).T[:1]
        for part in thirds(line):
            lines += [part[:, at : at + LANES] for at in range(0, rows, LANES)]
    lines.append(jnp.zeros((TAIL - len(lines), LANES), jnp.float32))
    tail = jnp.concatenate(lines, axis=0).astype(jnp.bfloat16)
    for out, place in zip(outs, slices_of(outs_of)):
        at = pl.multiple_of(place * width, width)
        out[:rows, :] = total_sums[:, pl.ds(at, width)].astype(jnp.bfloat16)
        out[rows:, :LANES] = tail


def attend(pieces, steps, begun, cache, latent, outs_of, scale):
    rows, count = begun.shape[0], max(len(outs_of), 1)
    return pl.pallas_call(
        functools.partial(attend_kernel, steps=steps, outs_of=outs_of, scale=scale),
        out_shape=[jax.ShapeDtypeStruct((rows + TAIL, latent // count), jnp.bfloat16)] * count,
        in_specs=[VMEM] * (len(pieces) + 2),
        out_specs=[VMEM] * count,
        scratch_shapes=[pltpu.VMEM((rows, latent), jnp.float32)],
        compiler_params=pltpu.CompilerParams(vmem_limit_bytes=11 * MIB),
        name="attend",
    )(*pieces, begun, cache)


def numbers_of(tail, rows):
    each = rows // LANES
    tail = tail.astype(jnp.float32)
    found = []
    for first in (0, 3 * each):
        parts = [
            jnp.concatenate([tail[at + i : at + i + 1] for i in range(each)], axis=1)
            for at in range(first, first + 3 * each, each)
        ]
        found.append(parts[0] + parts[1] + parts[2])
    return found


def keep_kernel(block, out):
    out[...] = block[...]


def keep(block):
    return pl.pallas_call(
        keep_kernel,
        out_shape=jax.ShapeDtypeStruct(block.shape, block.dtype),
        in_specs=[VMEM],
        out_specs=VMEM,
        compiler_params=pltpu.CompilerParams(vmem_limit_bytes=1 * MIB),
        cost_estimate=spans(40),
        name="keep",
    )(block)


def values_kernel(*refs, drafts):
    blocks, (value_absorb, out, found) = refs[:-3], refs[-3:]
    rows = out.shape[0]
    heads, width, value_width = value_absorb.shape
    numbers = [numbers_of(block[rows:, :], rows) for block in blocks]
    top = functools.reduce(jnp.maximum, [number[0] for number in numbers])
    factors = [jnp.exp(number[0] - top) for number in numbers]
    total = sum(factor * number[1] for factor, number in zip(factors, numbers))
    latent = jnp.zeros((rows, width), jnp.float32)
    for block, factor in zip(blocks, factors):
        column = jnp.broadcast_to(factor / total, (width, rows)).T
        latent += block[:rows, :].astype(jnp.float32) * column
    pair_products(latent, value_absorb, 0, heads, drafts, found)
    out[...] = found[...].astype(out.dtype)


def values_of(blocks, value_absorb, drafts):
    rows = blocks[0].shape[0] - TAIL
    return pl.pallas_call(
        functools.partial(values_kernel, drafts=drafts),
        out_shape=jax.ShapeDtypeStruct((rows, value_absorb.shape[2]), jnp.bfloat16),
        in_specs=[VMEM] * (len(blocks) + 1),
        out_specs=VMEM,
        scratch_shapes=[pltpu.VMEM((rows, value_absorb.shape[2]), jnp.float32)],
        compiler_params=pltpu.CompilerParams(vmem_limit_bytes=8 * MIB),
        name="values",
    )(*blocks, value_absorb)


def half_of(weight, other):
    half = weight.shape[1] // 2
    me = lax.axis_index("head")
    at = pl.multiple_of((1 - me if other else me) * half, half)
    return weight[:, pl.ds(at, half)]


def theirs_kernel(*refs, drafts):
    partials, (weight, theirs, flat, rows_ref) = refs[:-4], refs[-4:]
    rows, value_width = partials[0].shape
    summed = sum(partial[...].astype(jnp.float32) for partial in partials)
    for head in range(rows // drafts):
        rows_ref[:, head * value_width : (head + 1) * value_width] = summed[
            head * drafts : (head + 1) * drafts
        ]
    flat[...] = rows_ref[...].astype(jnp.bfloat16)
    theirs[...] = jnp.dot(flat[...], half_of(weight, True), preferred_element_type=jnp.float32)


def theirs_of(partials, weight, drafts):
    depth, width = weight.shape
    return pl.pallas_call(
        functools.partial(theirs_kernel, drafts=drafts),
        out_shape=[
            jax.ShapeDtypeStruct((drafts, width // 2), jnp.float32),
            jax.ShapeDtypeStruct((drafts, depth), jnp.bfloat16),
        ],
        in_specs=[VMEM] * (len(partials) + 1),
        out_specs=[VMEM] * 2,
        scratch_shapes=[pltpu.VMEM((drafts, depth), jnp.float32)],
        compiler_params=pltpu.CompilerParams(vmem_limit_bytes=4 * MIB),
        name="theirs",
    )(*partials, weight)


def mine_kernel(flat, weight, mine):
    mine[...] = jnp.dot(flat[...], half_of(weight, False), preferred_element_type=jnp.float32)


def mine_of(flat, weight):
    return pl.pallas_call(
        mine_kernel,
        out_shape=jax.ShapeDtypeStruct((flat.shape[0], weight.shape[1] // 2), jnp.float32),
        in_specs=[VMEM] * 2,
        out_specs=VMEM,
        compiler_params=pltpu.CompilerParams(vmem_limit_bytes=4 * MIB),
        cost_estimate=spans(2),
        name="mine",
    )(flat, weight)


def combine_many(block, rows):
    top, total = (line[0] for line in numbers_of(block[rows:, :LANES], rows))
    joint = lax.pmax(top, "ctx")
    factor = jnp.exp(top - joint)
    total = lax.psum(total * factor, "ctx")
    weighted = block[:rows].astype(jnp.float32) * factor[:, None]
    summed = lax.psum_scatter(weighted, "ctx", scatter_dimension=1, tiled=True)
    return (summed / total[:, None]).astype(jnp.bfloat16)


def local(
    query_nope,
    query_rope,
    latent_cache,
    lengths,
    block_ids,
    key_absorb,
    value_absorb,
    output_weight,
):
    _, drafts, heads, nope = query_nope.shape
    rope = query_rope.shape[3]
    tokens = latent_cache.shape[1]
    scale = (nope + rope) ** (-0.5)
    rows, latent = drafts * heads, latent_cache.shape[2] - rope
    peers = lax.axis_size("ctx")
    few = peers == PEERS and lax.axis_size("head") == 2 and key_absorb.shape[2] == LANES

    q_piece = queries_of(query_nope[0], key_absorb)
    bias, rope_rows = prepare(lengths, block_ids[0], query_rope[0], tokens)
    cache = latent_cache[0].T
    if few:
        steps = tuple(range(peers))
        pieces = [q_piece] + [swap(q_piece, "ctx", step) for step in steps[1:]]
        early, late = (0, 1), (2, 3)
        begun = begin([pieces[step] for step in early], early, rope_rows, cache, bias)
        blocks = attend(
            [pieces[step] for step in late], late, begun, cache, latent, steps, scale
        )
        blocks = [keep(blocks[0])] + [swap(blocks[step], "ctx", step) for step in (2, 3, 1)]
        partial = values_of(blocks, value_absorb, drafts)
        partials = [partial] + [turn(partial, "ctx", step) for step in (2, 1, 3)]
        theirs, flat = theirs_of(partials, output_weight, drafts)
        summed = mine_of(flat, output_weight) + swap(theirs, "head", 1)
    else:
        queries = lax.all_gather(q_piece, "ctx", axis=1, tiled=True)
        begun = begin([queries], (), rope_rows, cache, bias)
        block = attend([], (), begun, cache, latent, (), scale)[0]
        o_latent = combine_many(block, rows)
        head_values = jnp.einsum(
            "htc,hcv->thv",
            o_latent.reshape(heads, drafts, -1),
            value_absorb,
            preferred_element_type=jnp.float32,
        )
        head_values = lax.psum(head_values, "ctx").astype(jnp.bfloat16)
        found = jnp.dot(
            head_values.reshape(drafts, -1), output_weight, preferred_element_type=jnp.float32
        )
        summed = lax.psum_scatter(found, "head", scatter_dimension=1, tiled=True)
    return summed.astype(jnp.bfloat16)[None]


def solution(mesh):
    placed = (
        P(("groups", "sub"), None, "head", None),
        P(("groups", "sub"), None, "head", None),
        P(("groups", "sub"), "ctx", None),
        P(("groups", "sub")),
        P(("groups", "sub"), None, None),
        P("head", None, "ctx"),
        P("head", "ctx", None),
        P("head", "ctx"),
    )
    return jax.shard_map(
        local,
        mesh=mesh,
        in_specs=placed,
        out_specs=P(("groups", "sub"), None, ("ctx", "head")),
        check_vma=False,
    )
```

```python
import functools

import jax
import jax.numpy as jnp
from jax import lax
from jax.experimental import pallas as pl
from jax.experimental.pallas import tpu as pltpu
from jax.sharding import PartitionSpec as P

BLK = 64
PEERS = 4
LANES = 128
CHUNK = 256
TAIL = 16
LOG2E = 1.4426950408889634
HIDDEN = -1e30
MIB = 1024 * 1024
VMEM = pl.BlockSpec(memory_space=pltpu.VMEM)
HBM = pl.BlockSpec(memory_space=pltpu.HBM)


def spans(microseconds):
    return pl.CostEstimate(flops=int(microseconds * 1e9), bytes_accessed=0, transcendentals=0)


def swap(value, axis, step):
    count = lax.axis_size(axis)
    return lax.ppermute(value, axis, [(i, i ^ step) for i in range(count)])


def turn(value, axis, step):
    order = (0, 1, 3, 2)
    return lax.ppermute(value, axis, [(order[i], order[(i + step) % 4]) for i in range(4)])


def thirds(value):
    high = value.astype(jnp.bfloat16)
    rest = value - high.astype(jnp.float32)
    middle = rest.astype(jnp.bfloat16)
    low = (rest - middle.astype(jnp.float32)).astype(jnp.bfloat16)
    return [part.astype(jnp.float32) for part in (high, middle, low)]


def by_head(value, rows_ref):
    drafts, heads, _ = value.shape
    for draft in range(drafts):
        rows_ref[pl.ds(draft, heads, stride=drafts), :] = value[draft].astype(jnp.float32)


def pair_products(left, heads, first, last, drafts, store):
    pair, width = 2 * drafts, heads.shape[2]
    upper = lax.broadcasted_iota(jnp.int32, (pair, width), 0) < drafts
    for head in range(first, last, 2):
        both = jnp.concatenate([heads[head], heads[head + 1]], axis=1)
        at = slice(head * drafts, head * drafts + pair)
        found = jnp.dot(
            left[at].astype(jnp.bfloat16), both, preferred_element_type=jnp.float32
        )
        store[at, :] = jnp.where(upper, found[:, :width], found[:, width:])


def queries_kernel(query, key_absorb, out, query_here, held, rows_ref, found, arrived):
    drafts, heads, _ = query.shape
    parts = arrived.shape[0] - 1
    each = heads // parts
    copies = [pltpu.make_async_copy(query, query_here, arrived.at[parts])]
    for i in range(parts):
        at = pl.ds(i * each, each)
        copies.append(pltpu.make_async_copy(key_absorb.at[at], held.at[at], arrived.at[i]))
    for copy in copies:
        copy.start()
    copies[0].wait()
    by_head(query_here[...], rows_ref)
    left = rows_ref[...]
    for i in range(parts):
        copies[1 + i].wait()
        pair_products(left, held, i * each, (i + 1) * each, drafts, found)
    out[...] = found[...].astype(out.dtype)


def queries_of(query, key_absorb):
    drafts, heads, nope = query.shape
    rows, width = drafts * heads, key_absorb.shape[2]
    return pl.pallas_call(
        queries_kernel,
        out_shape=pltpu.VMEM((rows, width), jnp.bfloat16),
        in_specs=[HBM] * 2,
        out_specs=VMEM,
        scratch_shapes=[
            pltpu.VMEM(query.shape, query.dtype),
            pltpu.VMEM(key_absorb.shape, key_absorb.dtype),
            pltpu.VMEM((rows, nope), jnp.float32),
            pltpu.VMEM((rows, width), jnp.float32),
            pltpu.SemaphoreType.DMA((min(4, heads // 2) + 1,)),
        ],
        compiler_params=pltpu.CompilerParams(vmem_limit_bytes=60 * MIB),
        cost_estimate=spans(5),
        name="queries",
    )(query, key_absorb)


def prepare_kernel(
    lengths, block_ids, query_rope, bias, rope_out, rows_ref
):
    drafts, chosen = block_ids.shape
    tokens = bias.shape[1]
    ids = jnp.concatenate([block_ids[...]] * (8 // drafts), axis=0)
    position = lax.axis_index("ctx") * tokens + lax.broadcasted_iota(jnp.int32, (8, tokens), 1)
    block = position // BLK
    found = block == ids[:, :1]
    for i in range(1, chosen):
        found |= block == ids[:, i : i + 1]
    draft = lax.broadcasted_iota(jnp.int32, (8, tokens), 0) % drafts
    visible = found & (position <= lengths[0] - drafts + draft)
    bias[...] = jnp.where(visible, 0.0, HIDDEN)
    by_head(query_rope[...], rows_ref)
    rope_out[...] = rows_ref[...].astype(jnp.bfloat16)


def prepare(lengths, block_ids, query_rope, tokens):
    drafts, heads, rope = query_rope.shape
    return pl.pallas_call(
        prepare_kernel,
        out_shape=[
            jax.ShapeDtypeStruct((8, tokens), jnp.float32),
            jax.ShapeDtypeStruct((drafts * heads, rope), jnp.bfloat16),
        ],
        in_specs=[pl.BlockSpec(memory_space=pltpu.SMEM), VMEM, VMEM],
        out_specs=[VMEM] * 2,
        scratch_shapes=[pltpu.VMEM((drafts * heads, rope), jnp.float32)],
        compiler_params=pltpu.CompilerParams(vmem_limit_bytes=4 * MIB),
        cost_estimate=spans(12),
        name="prepare",
    )(lengths, block_ids, query_rope)


def rows_at(ref, places, width):
    found = [ref[pl.ds(pl.multiple_of(place * width, width), width), :] for place in places]
    return found[0] if len(found) == 1 else jnp.concatenate(found, axis=0)


def slices_of(steps):
    return [lax.axis_index("ctx") ^ step for step in steps] if steps else [0]


def on_ring(steps):
    if not steps:
        return [0]
    me = lax.axis_index("ctx")
    spot = me ^ (me >> 1)
    spots = [(spot + step) & 3 for step in steps]
    return [there ^ (there >> 1) for there in spots]


def begin_kernel(*refs, steps):
    pieces, (rope, cache, bias, scores) = refs[:-4], refs[-4:]
    rows, width = pieces[0].shape
    depth, tokens = cache.shape
    found = jnp.dot(
        jnp.concatenate([piece[...] for piece in pieces], axis=1),
        rows_at(cache, slices_of(steps), width),
        preferred_element_type=jnp.float32,
    )
    found += jnp.dot(
        rope[...], cache[depth - rope.shape[1] :, :], preferred_element_type=jnp.float32
    )
    scores[...] = (found.reshape(rows // 8, 8, tokens) + bias[...][None]).reshape(rows, tokens)


def begin(pieces, steps, rope, cache, bias):
    rows, tokens = pieces[0].shape[0], cache.shape[1]
    return pl.pallas_call(
        functools.partial(begin_kernel, steps=steps),
        out_shape=jax.ShapeDtypeStruct((rows, tokens), jnp.float32),
        in_specs=[VMEM] * (len(pieces) + 3),
        out_specs=VMEM,
        compiler_params=pltpu.CompilerParams(vmem_limit_bytes=6 * MIB),
        name="begin",
    )(*pieces, rope, cache, bias)


def attend_kernel(*refs, steps, outs_of, scale):
    pieces, (begun, cache) = refs[: len(steps)], refs[len(steps) : len(steps) + 2]
    outs, total_sums = refs[len(steps) + 2 : -1], refs[-1]
    rows, latent = total_sums.shape
    width = latent // len(outs)
    scores = begun[...]
    if steps:
        scores += jnp.dot(
            jnp.concatenate([piece[...] for piece in pieces], axis=1),
            rows_at(cache, slices_of(steps), width),
            preferred_element_type=jnp.float32,
        )
    top = jnp.max(scores, axis=1, keepdims=True)
    tokens = scores.shape[1]
    total = jnp.zeros((rows, 1), jnp.float32)
    sums = jnp.zeros((rows, latent), jnp.float32)
    for first in range(0, tokens, CHUNK):
        at = slice(first, first + CHUNK)
        weights = jnp.exp2((scores[:, at] - top) * (scale * LOG2E))
        total += jnp.sum(weights, axis=1, keepdims=True)
        sums += lax.dot_general(
            weights.astype(jnp.bfloat16),
            cache[:latent, at],
            (((1,), (1,)), ((), ())),
            preferred_element_type=jnp.float32,
        )
    total_sums[...] = sums

    lines = []
    for value in (top * scale, total):
        line = jnp.broadcast_to(value, (rows, LANES)).T[:1]
        for part in thirds(line):
            lines += [part[:, at : at + LANES] for at in range(0, rows, LANES)]
    lines.append(jnp.zeros((TAIL - len(lines), LANES), jnp.float32))
    tail = jnp.concatenate(lines, axis=0).astype(jnp.bfloat16)
    for out, place in zip(outs, on_ring(outs_of)):
        at = pl.multiple_of(place * width, width)
        out[:rows, :] = total_sums[:, pl.ds(at, width)].astype(jnp.bfloat16)
        out[rows:, :LANES] = tail


def attend(pieces, steps, begun, cache, latent, outs_of, scale):
    rows, count = begun.shape[0], max(len(outs_of), 1)
    return pl.pallas_call(
        functools.partial(attend_kernel, steps=steps, outs_of=outs_of, scale=scale),
        out_shape=[jax.ShapeDtypeStruct((rows + TAIL, latent // count), jnp.bfloat16)] * count,
        in_specs=[VMEM] * (len(pieces) + 2),
        out_specs=[VMEM] * count,
        scratch_shapes=[pltpu.VMEM((rows, latent), jnp.float32)],
        compiler_params=pltpu.CompilerParams(vmem_limit_bytes=11 * MIB),
        name="attend",
    )(*pieces, begun, cache)


def numbers_of(tail, rows):
    each = rows // LANES
    tail = tail.astype(jnp.float32)
    found = []
    for first in (0, 3 * each):
        parts = [
            jnp.concatenate([tail[at + i : at + i + 1] for i in range(each)], axis=1)
            for at in range(first, first + 3 * each, each)
        ]
        found.append(parts[0] + parts[1] + parts[2])
    return found


def keep_kernel(block, out):
    out[...] = block[...]


def keep(block):
    return pl.pallas_call(
        keep_kernel,
        out_shape=jax.ShapeDtypeStruct(block.shape, block.dtype),
        in_specs=[VMEM],
        out_specs=VMEM,
        compiler_params=pltpu.CompilerParams(vmem_limit_bytes=1 * MIB),
        cost_estimate=spans(40),
        name="keep",
    )(block)


def values_kernel(*refs, drafts):
    blocks, (value_absorb, out, found) = refs[:-3], refs[-3:]
    rows = out.shape[0]
    heads, width, value_width = value_absorb.shape
    numbers = [numbers_of(block[rows:, :], rows) for block in blocks]
    top = functools.reduce(jnp.maximum, [number[0] for number in numbers])
    factors = [jnp.exp(number[0] - top) for number in numbers]
    total = sum(factor * number[1] for factor, number in zip(factors, numbers))
    latent = jnp.zeros((rows, width), jnp.float32)
    for block, factor in zip(blocks, factors):
        column = jnp.broadcast_to(factor / total, (width, rows)).T
        latent += block[:rows, :].astype(jnp.float32) * column
    pair_products(latent, value_absorb, 0, heads, drafts, found)
    out[...] = found[...].astype(out.dtype)


def values_of(blocks, value_absorb, drafts):
    rows = blocks[0].shape[0] - TAIL
    return pl.pallas_call(
        functools.partial(values_kernel, drafts=drafts),
        out_shape=jax.ShapeDtypeStruct((rows, value_absorb.shape[2]), jnp.bfloat16),
        in_specs=[VMEM] * (len(blocks) + 1),
        out_specs=VMEM,
        scratch_shapes=[pltpu.VMEM((rows, value_absorb.shape[2]), jnp.float32)],
        compiler_params=pltpu.CompilerParams(vmem_limit_bytes=8 * MIB),
        name="values",
    )(*blocks, value_absorb)


def half_of(weight, other):
    half = weight.shape[1] // 2
    me = lax.axis_index("head")
    at = pl.multiple_of((1 - me if other else me) * half, half)
    return weight[:, pl.ds(at, half)]


def theirs_kernel(*refs, drafts):
    partials, (weight, theirs, flat, rows_ref) = refs[:-4], refs[-4:]
    rows, value_width = partials[0].shape
    summed = sum(partial[...].astype(jnp.float32) for partial in partials)
    for head in range(rows // drafts):
        rows_ref[:, head * value_width : (head + 1) * value_width] = summed[
            head * drafts : (head + 1) * drafts
        ]
    flat[...] = rows_ref[...].astype(jnp.bfloat16)
    theirs[...] = jnp.dot(flat[...], half_of(weight, True), preferred_element_type=jnp.float32)


def theirs_of(partials, weight, drafts):
    depth, width = weight.shape
    return pl.pallas_call(
        functools.partial(theirs_kernel, drafts=drafts),
        out_shape=[
            jax.ShapeDtypeStruct((drafts, width // 2), jnp.float32),
            jax.ShapeDtypeStruct((drafts, depth), jnp.bfloat16),
        ],
        in_specs=[VMEM] * (len(partials) + 1),
        out_specs=[VMEM] * 2,
        scratch_shapes=[pltpu.VMEM((drafts, depth), jnp.float32)],
        compiler_params=pltpu.CompilerParams(vmem_limit_bytes=4 * MIB),
        name="theirs",
    )(*partials, weight)


def mine_kernel(flat, weight, mine):
    mine[...] = jnp.dot(flat[...], half_of(weight, False), preferred_element_type=jnp.float32)


def mine_of(flat, weight):
    return pl.pallas_call(
        mine_kernel,
        out_shape=jax.ShapeDtypeStruct((flat.shape[0], weight.shape[1] // 2), jnp.float32),
        in_specs=[VMEM] * 2,
        out_specs=VMEM,
        compiler_params=pltpu.CompilerParams(vmem_limit_bytes=4 * MIB),
        cost_estimate=spans(2),
        name="mine",
    )(flat, weight)


def combine_many(block, rows):
    top, total = (line[0] for line in numbers_of(block[rows:, :LANES], rows))
    joint = lax.pmax(top, "ctx")
    factor = jnp.exp(top - joint)
    total = lax.psum(total * factor, "ctx")
    weighted = block[:rows].astype(jnp.float32) * factor[:, None]
    summed = lax.psum_scatter(weighted, "ctx", scatter_dimension=1, tiled=True)
    return (summed / total[:, None]).astype(jnp.bfloat16)


def local(
    query_nope,
    query_rope,
    latent_cache,
    lengths,
    block_ids,
    key_absorb,
    value_absorb,
    output_weight,
):
    _, drafts, heads, nope = query_nope.shape
    rope = query_rope.shape[3]
    tokens = latent_cache.shape[1]
    scale = (nope + rope) ** (-0.5)
    rows, latent = drafts * heads, latent_cache.shape[2] - rope
    peers = lax.axis_size("ctx")
    few = peers == PEERS and lax.axis_size("head") == 2 and key_absorb.shape[2] == LANES

    q_piece = queries_of(query_nope[0], key_absorb)
    bias, rope_rows = prepare(lengths, block_ids[0], query_rope[0], tokens)
    cache = latent_cache[0].T
    if few:
        steps = tuple(range(peers))
        pieces = [q_piece] + [swap(q_piece, "ctx", step) for step in steps[1:]]
        early, late = (0, 1), (2, 3)
        begun = begin([pieces[step] for step in early], early, rope_rows, cache, bias)
        blocks = attend(
            [pieces[step] for step in late], late, begun, cache, latent, steps, scale
        )
        blocks = [keep(blocks[0])] + [turn(blocks[step], "ctx", step) for step in (1, 2, 3)]
        partial = values_of(blocks, value_absorb, drafts)
        partials = [partial] + [turn(partial, "ctx", step) for step in (2, 1, 3)]
        theirs, flat = theirs_of(partials, output_weight, drafts)
        summed = mine_of(flat, output_weight) + swap(theirs, "head", 1)
    else:
        queries = lax.all_gather(q_piece, "ctx", axis=1, tiled=True)
        begun = begin([queries], (), rope_rows, cache, bias)
        block = attend([], (), begun, cache, latent, (), scale)[0]
        o_latent = combine_many(block, rows)
        head_values = jnp.einsum(
            "htc,hcv->thv",
            o_latent.reshape(heads, drafts, -1),
            value_absorb,
            preferred_element_type=jnp.float32,
        )
        head_values = lax.psum(head_values, "ctx").astype(jnp.bfloat16)
        found = jnp.dot(
            head_values.reshape(drafts, -1), output_weight, preferred_element_type=jnp.float32
        )
        summed = lax.psum_scatter(found, "head", scatter_dimension=1, tiled=True)
    return summed.astype(jnp.bfloat16)[None]


def solution(mesh):
    placed = (
        P(("groups", "sub"), None, "head", None),
        P(("groups", "sub"), None, "head", None),
        P(("groups", "sub"), "ctx", None),
        P(("groups", "sub")),
        P(("groups", "sub"), None, None),
        P("head", None, "ctx"),
        P("head", "ctx", None),
        P("head", "ctx"),
    )
    return jax.shard_map(
        local,
        mesh=mesh,
        in_specs=placed,
        out_specs=P(("groups", "sub"), None, ("ctx", "head")),
        check_vma=False,
    )
```

```python
import functools

import jax
import jax.numpy as jnp
from jax import lax
from jax.experimental import pallas as pl
from jax.experimental.pallas import tpu as pltpu
from jax.sharding import PartitionSpec as P

BLK = 64
PEERS = 4
LANES = 128
CHUNK = 256
TAIL = 16
LOG2E = 1.4426950408889634
HIDDEN = -1e30
MIB = 1024 * 1024
VMEM = pl.BlockSpec(memory_space=pltpu.VMEM)
HBM = pl.BlockSpec(memory_space=pltpu.HBM)


def spans(microseconds):
    return pl.CostEstimate(flops=int(microseconds * 1e9), bytes_accessed=0, transcendentals=0)


def swap(value, axis, step):
    count = lax.axis_size(axis)
    return lax.ppermute(value, axis, [(i, i ^ step) for i in range(count)])


def turn(value, axis, step):
    order = (0, 1, 3, 2)
    return lax.ppermute(value, axis, [(order[i], order[(i + step) % 4]) for i in range(4)])


def thirds(value):
    high = value.astype(jnp.bfloat16)
    rest = value - high.astype(jnp.float32)
    middle = rest.astype(jnp.bfloat16)
    low = (rest - middle.astype(jnp.float32)).astype(jnp.bfloat16)
    return [part.astype(jnp.float32) for part in (high, middle, low)]


def by_head(value, rows_ref):
    drafts, heads, _ = value.shape
    for draft in range(drafts):
        rows_ref[pl.ds(draft, heads, stride=drafts), :] = value[draft].astype(jnp.float32)


def pair_products(left, heads, first, last, drafts, store):
    pair, width = 2 * drafts, heads.shape[2]
    upper = lax.broadcasted_iota(jnp.int32, (pair, width), 0) < drafts
    for head in range(first, last, 2):
        both = jnp.concatenate([heads[head], heads[head + 1]], axis=1)
        at = slice(head * drafts, head * drafts + pair)
        found = jnp.dot(
            left[at].astype(jnp.bfloat16), both, preferred_element_type=jnp.float32
        )
        store[at, :] = jnp.where(upper, found[:, :width], found[:, width:])


def queries_kernel(query, key_absorb, out, query_here, held, rows_ref, found, arrived):
    drafts, heads, _ = query.shape
    parts = arrived.shape[0] - 1
    each = heads // parts
    copies = [pltpu.make_async_copy(query, query_here, arrived.at[parts])]
    for i in range(parts):
        at = pl.ds(i * each, each)
        copies.append(pltpu.make_async_copy(key_absorb.at[at], held.at[at], arrived.at[i]))
    for copy in copies:
        copy.start()
    copies[0].wait()
    by_head(query_here[...], rows_ref)
    left = rows_ref[...]
    for i in range(parts):
        copies[1 + i].wait()
        pair_products(left, held, i * each, (i + 1) * each, drafts, found)
    out[...] = found[...].astype(out.dtype)


def queries_of(query, key_absorb):
    drafts, heads, nope = query.shape
    rows, width = drafts * heads, key_absorb.shape[2]
    return pl.pallas_call(
        queries_kernel,
        out_shape=pltpu.VMEM((rows, width), jnp.bfloat16),
        in_specs=[HBM] * 2,
        out_specs=VMEM,
        scratch_shapes=[
            pltpu.VMEM(query.shape, query.dtype),
            pltpu.VMEM(key_absorb.shape, key_absorb.dtype),
            pltpu.VMEM((rows, nope), jnp.float32),
            pltpu.VMEM((rows, width), jnp.float32),
            pltpu.SemaphoreType.DMA((min(4, heads // 2) + 1,)),
        ],
        compiler_params=pltpu.CompilerParams(vmem_limit_bytes=60 * MIB),
        cost_estimate=spans(5),
        name="queries",
    )(query, key_absorb)


def prepare_kernel(
    lengths, block_ids, query_rope, bias, rope_out, rows_ref
):
    drafts, chosen = block_ids.shape
    tokens = bias.shape[1]
    ids = jnp.concatenate([block_ids[...]] * (8 // drafts), axis=0)
    position = lax.axis_index("ctx") * tokens + lax.broadcasted_iota(jnp.int32, (8, tokens), 1)
    block = position // BLK
    found = block == ids[:, :1]
    for i in range(1, chosen):
        found |= block == ids[:, i : i + 1]
    draft = lax.broadcasted_iota(jnp.int32, (8, tokens), 0) % drafts
    visible = found & (position <= lengths[0] - drafts + draft)
    bias[...] = jnp.where(visible, 0.0, HIDDEN)
    by_head(query_rope[...], rows_ref)
    rope_out[...] = rows_ref[...].astype(jnp.bfloat16)


def prepare(lengths, block_ids, query_rope, tokens):
    drafts, heads, rope = query_rope.shape
    return pl.pallas_call(
        prepare_kernel,
        out_shape=[
            jax.ShapeDtypeStruct((8, tokens), jnp.float32),
            jax.ShapeDtypeStruct((drafts * heads, rope), jnp.bfloat16),
        ],
        in_specs=[pl.BlockSpec(memory_space=pltpu.SMEM), VMEM, VMEM],
        out_specs=[VMEM] * 2,
        scratch_shapes=[pltpu.VMEM((drafts * heads, rope), jnp.float32)],
        compiler_params=pltpu.CompilerParams(vmem_limit_bytes=4 * MIB),
        cost_estimate=spans(12),
        name="prepare",
    )(lengths, block_ids, query_rope)


def rows_at(ref, places, width):
    found = [ref[pl.ds(pl.multiple_of(place * width, width), width), :] for place in places]
    return found[0] if len(found) == 1 else jnp.concatenate(found, axis=0)


def slices_of(steps):
    return [lax.axis_index("ctx") ^ step for step in steps] if steps else [0]


def on_ring(steps):
    if not steps:
        return [0]
    me = lax.axis_index("ctx")
    spot = me ^ (me >> 1)
    spots = [(spot + step) & 3 for step in steps]
    return [there ^ (there >> 1) for there in spots]


def begin_kernel(*refs, steps):
    pieces, (rope, cache, bias, scores) = refs[:-4], refs[-4:]
    rows, width = pieces[0].shape
    depth, tokens = cache.shape
    found = jnp.dot(
        jnp.concatenate([piece[...] for piece in pieces], axis=1),
        rows_at(cache, slices_of(steps), width),
        preferred_element_type=jnp.float32,
    )
    found += jnp.dot(
        rope[...], cache[depth - rope.shape[1] :, :], preferred_element_type=jnp.float32
    )
    scores[...] = (found.reshape(rows // 8, 8, tokens) + bias[...][None]).reshape(rows, tokens)


def begin(pieces, steps, rope, cache, bias):
    rows, tokens = pieces[0].shape[0], cache.shape[1]
    return pl.pallas_call(
        functools.partial(begin_kernel, steps=steps),
        out_shape=jax.ShapeDtypeStruct((rows, tokens), jnp.float32),
        in_specs=[VMEM] * (len(pieces) + 3),
        out_specs=VMEM,
        compiler_params=pltpu.CompilerParams(vmem_limit_bytes=6 * MIB),
        name="begin",
    )(*pieces, rope, cache, bias)


def attend_kernel(*refs, steps, outs_of, scale):
    pieces, (begun, cache) = refs[: len(steps)], refs[len(steps) : len(steps) + 2]
    outs, total_sums = refs[len(steps) + 2 : -1], refs[-1]
    rows, latent = total_sums.shape
    width = latent // len(outs)
    left = jnp.concatenate([piece[...] for piece in pieces], axis=1) if steps else None
    right = rows_at(cache, slices_of(steps), width) if steps else None
    found = []
    for first in range(0, begun.shape[1], 1024):
        part = begun[:, first : first + 1024]
        if steps:
            part += jnp.dot(
                left, right[:, first : first + 1024], preferred_element_type=jnp.float32
            )
        found.append(part)
    scores = jnp.concatenate(found, axis=1)
    top = jnp.max(scores, axis=1, keepdims=True)
    tokens = scores.shape[1]
    total = jnp.zeros((rows, 1), jnp.float32)
    sums = jnp.zeros((rows, latent), jnp.float32)
    for first in range(0, tokens, CHUNK):
        at = slice(first, first + CHUNK)
        weights = jnp.exp2((scores[:, at] - top) * (scale * LOG2E))
        total += jnp.sum(weights, axis=1, keepdims=True)
        sums += lax.dot_general(
            weights.astype(jnp.bfloat16),
            cache[:latent, at],
            (((1,), (1,)), ((), ())),
            preferred_element_type=jnp.float32,
        )
    total_sums[...] = sums

    lines = []
    for value in (top * scale, total):
        line = jnp.broadcast_to(value, (rows, LANES)).T[:1]
        for part in thirds(line):
            lines += [part[:, at : at + LANES] for at in range(0, rows, LANES)]
    lines.append(jnp.zeros((TAIL - len(lines), LANES), jnp.float32))
    tail = jnp.concatenate(lines, axis=0).astype(jnp.bfloat16)
    for out, place in zip(outs, on_ring(outs_of)):
        at = pl.multiple_of(place * width, width)
        out[:rows, :] = total_sums[:, pl.ds(at, width)].astype(jnp.bfloat16)
        out[rows:, :LANES] = tail


def attend(pieces, steps, begun, cache, latent, outs_of, scale):
    rows, count = begun.shape[0], max(len(outs_of), 1)
    return pl.pallas_call(
        functools.partial(attend_kernel, steps=steps, outs_of=outs_of, scale=scale),
        out_shape=[jax.ShapeDtypeStruct((rows + TAIL, latent // count), jnp.bfloat16)] * count,
        in_specs=[VMEM] * (len(pieces) + 2),
        out_specs=[VMEM] * count,
        scratch_shapes=[pltpu.VMEM((rows, latent), jnp.float32)],
        compiler_params=pltpu.CompilerParams(vmem_limit_bytes=11 * MIB),
        name="attend",
    )(*pieces, begun, cache)


def numbers_of(tail, rows):
    each = rows // LANES
    tail = tail.astype(jnp.float32)
    found = []
    for first in (0, 3 * each):
        parts = [
            jnp.concatenate([tail[at + i : at + i + 1] for i in range(each)], axis=1)
            for at in range(first, first + 3 * each, each)
        ]
        found.append(parts[0] + parts[1] + parts[2])
    return found


def keep_kernel(block, out):
    out[...] = block[...]


def keep(block):
    return pl.pallas_call(
        keep_kernel,
        out_shape=jax.ShapeDtypeStruct(block.shape, block.dtype),
        in_specs=[VMEM],
        out_specs=VMEM,
        compiler_params=pltpu.CompilerParams(vmem_limit_bytes=1 * MIB),
        cost_estimate=spans(40),
        name="keep",
    )(block)


def values_kernel(*refs, drafts):
    blocks, (value_absorb, out, found) = refs[:-3], refs[-3:]
    rows = out.shape[0]
    heads, width, value_width = value_absorb.shape
    numbers = [numbers_of(block[rows:, :], rows) for block in blocks]
    top = functools.reduce(jnp.maximum, [number[0] for number in numbers])
    factors = [jnp.exp(number[0] - top) for number in numbers]
    total = sum(factor * number[1] for factor, number in zip(factors, numbers))
    latent = jnp.zeros((rows, width), jnp.float32)
    for block, factor in zip(blocks, factors):
        column = jnp.broadcast_to(factor / total, (width, rows)).T
        latent += block[:rows, :].astype(jnp.float32) * column
    pair_products(latent, value_absorb, 0, heads, drafts, found)
    out[...] = found[...].astype(out.dtype)


def values_of(blocks, value_absorb, drafts):
    rows = blocks[0].shape[0] - TAIL
    return pl.pallas_call(
        functools.partial(values_kernel, drafts=drafts),
        out_shape=jax.ShapeDtypeStruct((rows, value_absorb.shape[2]), jnp.bfloat16),
        in_specs=[VMEM] * (len(blocks) + 1),
        out_specs=VMEM,
        scratch_shapes=[pltpu.VMEM((rows, value_absorb.shape[2]), jnp.float32)],
        compiler_params=pltpu.CompilerParams(vmem_limit_bytes=8 * MIB),
        name="values",
    )(*blocks, value_absorb)


def half_of(weight, other):
    half = weight.shape[1] // 2
    me = lax.axis_index("head")
    at = pl.multiple_of((1 - me if other else me) * half, half)
    return weight[:, pl.ds(at, half)]


def theirs_kernel(*refs, drafts):
    partials, (weight, theirs, flat, rows_ref) = refs[:-4], refs[-4:]
    rows, value_width = partials[0].shape
    summed = sum(partial[...].astype(jnp.float32) for partial in partials)
    for head in range(rows // drafts):
        rows_ref[:, head * value_width : (head + 1) * value_width] = summed[
            head * drafts : (head + 1) * drafts
        ]
    flat[...] = rows_ref[...].astype(jnp.bfloat16)
    theirs[...] = jnp.dot(flat[...], half_of(weight, True), preferred_element_type=jnp.float32)


def theirs_of(partials, weight, drafts):
    depth, width = weight.shape
    return pl.pallas_call(
        functools.partial(theirs_kernel, drafts=drafts),
        out_shape=[
            jax.ShapeDtypeStruct((drafts, width // 2), jnp.float32),
            jax.ShapeDtypeStruct((drafts, depth), jnp.bfloat16),
        ],
        in_specs=[VMEM] * (len(partials) + 1),
        out_specs=[VMEM] * 2,
        scratch_shapes=[pltpu.VMEM((drafts, depth), jnp.float32)],
        compiler_params=pltpu.CompilerParams(vmem_limit_bytes=4 * MIB),
        name="theirs",
    )(*partials, weight)


def mine_kernel(flat, weight, mine):
    mine[...] = jnp.dot(flat[...], half_of(weight, False), preferred_element_type=jnp.float32)


def mine_of(flat, weight):
    return pl.pallas_call(
        mine_kernel,
        out_shape=jax.ShapeDtypeStruct((flat.shape[0], weight.shape[1] // 2), jnp.float32),
        in_specs=[VMEM] * 2,
        out_specs=VMEM,
        compiler_params=pltpu.CompilerParams(vmem_limit_bytes=4 * MIB),
        cost_estimate=spans(2),
        name="mine",
    )(flat, weight)


def combine_many(block, rows):
    top, total = (line[0] for line in numbers_of(block[rows:, :LANES], rows))
    joint = lax.pmax(top, "ctx")
    factor = jnp.exp(top - joint)
    total = lax.psum(total * factor, "ctx")
    weighted = block[:rows].astype(jnp.float32) * factor[:, None]
    summed = lax.psum_scatter(weighted, "ctx", scatter_dimension=1, tiled=True)
    return (summed / total[:, None]).astype(jnp.bfloat16)


def local(
    query_nope,
    query_rope,
    latent_cache,
    lengths,
    block_ids,
    key_absorb,
    value_absorb,
    output_weight,
):
    _, drafts, heads, nope = query_nope.shape
    rope = query_rope.shape[3]
    tokens = latent_cache.shape[1]
    scale = (nope + rope) ** (-0.5)
    rows, latent = drafts * heads, latent_cache.shape[2] - rope
    peers = lax.axis_size("ctx")
    few = peers == PEERS and lax.axis_size("head") == 2 and key_absorb.shape[2] == LANES

    q_piece = queries_of(query_nope[0], key_absorb)
    bias, rope_rows = prepare(lengths, block_ids[0], query_rope[0], tokens)
    cache = latent_cache[0].T
    if few:
        steps = tuple(range(peers))
        pieces = [q_piece] + [swap(q_piece, "ctx", step) for step in steps[1:]]
        early, late = (0, 1), (2, 3)
        begun = begin([pieces[step] for step in early], early, rope_rows, cache, bias)
        blocks = attend(
            [pieces[step] for step in late], late, begun, cache, latent, steps, scale
        )
        blocks = [keep(blocks[0])] + [turn(blocks[step], "ctx", step) for step in (1, 2, 3)]
        partial = values_of(blocks, value_absorb, drafts)
        partials = [partial] + [turn(partial, "ctx", step) for step in (2, 1, 3)]
        theirs, flat = theirs_of(partials, output_weight, drafts)
        summed = mine_of(flat, output_weight) + swap(theirs, "head", 1)
    else:
        queries = lax.all_gather(q_piece, "ctx", axis=1, tiled=True)
        begun = begin([queries], (), rope_rows, cache, bias)
        block = attend([], (), begun, cache, latent, (), scale)[0]
        o_latent = combine_many(block, rows)
        head_values = jnp.einsum(
            "htc,hcv->thv",
            o_latent.reshape(heads, drafts, -1),
            value_absorb,
            preferred_element_type=jnp.float32,
        )
        head_values = lax.psum(head_values, "ctx").astype(jnp.bfloat16)
        found = jnp.dot(
            head_values.reshape(drafts, -1), output_weight, preferred_element_type=jnp.float32
        )
        summed = lax.psum_scatter(found, "head", scatter_dimension=1, tiled=True)
    return summed.astype(jnp.bfloat16)[None]


def solution(mesh):
    placed = (
        P(("groups", "sub"), None, "head", None),
        P(("groups", "sub"), None, "head", None),
        P(("groups", "sub"), "ctx", None),
        P(("groups", "sub")),
        P(("groups", "sub"), None, None),
        P("head", None, "ctx"),
        P("head", "ctx", None),
        P("head", "ctx"),
    )
    return jax.shard_map(
        local,
        mesh=mesh,
        in_specs=placed,
        out_specs=P(("groups", "sub"), None, ("ctx", "head")),
        check_vma=False,
    )
```
